32 devices in a mesh: dom: 4 (over y, x), dev: 8 (over z, core).
Axes of the slice: x: 2, y: 2, z: 4, core: 2. Of those that a mesh axis runs over, the one named last changes fastest.
Arguments:
- features: float32 [32768, 512], P(('dom', 'dev')), may hold values from -6 to 6
- tile_rows: int32 [2560], P(('dom', 'dev')), may hold values from 0 to 7
- tile_cols: int32 [2560], P(('dom', 'dev')), may hold values from 0 to 19
- tile_vals: float32 [2560, 128, 128], P(('dom', 'dev')), may hold values from -0.21875 to 0.21875
- tile_count: int32 [32], P(('dom', 'dev')), may hold values from 1 to 80, as said below
- near_send: int32 [32, 8, 1], P(('dom', 'dev')), may hold values from 0 to 7
- far_send: int32 [32, 2, 2], P(('dom', 'dev')), may hold values from 0 to 7
- skew_raw: float32 [2, 512, 512], replicated, may hold values from -0.25 to 0.25
Outputs:
- features_out: float32 [32768, 512], P(('dom', 'dev'))
The draws below stay inside these ranges and needn't reach their ends.
Inputs may be any that keep to these rules, and one draw needn't show every extreme that they name: The first tile_count[i] tile slots of device i are live, the others are ignored; some device holds 80 live tiles.
All inputs are finite; a program needn't handle non-finite values.
Results may differ from the reference program's by a relative error of at most 0.0001.
Values sent between devices are 32-bit elements; how exact they have to be, the bound alone decides.
No kernel may reach another device: no remote copies, remote signals or barrier semaphores. Data moves between devices by JAX's collectives and lax.ppermute only.
A program may use at most 128 MiB of HBM per device.

```python
import jax
import jax.numpy as jnp
from jax import lax

F = 512
TILE = 128
RB = 8
TILES_DEV = 80
CAP = 1
HCAP = 2
L = 2
POOL = 20
NODES = 32768
N_DOM = 4
N_DEV = 8
DEVICES = 32


def draw_tile_count(key, part):
    key = jax.random.fold_in(key, 7)
    first_key, second_key = jax.random.split(key)
    divisor = 1 + jax.random.randint(first_key, (DEVICES,), 0, 4)
    counts = TILES_DEV // divisor
    full_slot = jax.random.randint(second_key, (), 0, DEVICES)
    counts = counts.at[full_slot].set(TILES_DEV)
    return counts.astype(jnp.int32)


def with_ends(drawn, stream_key, smallest, high):
    place = [jax.random.randint(jax.random.fold_in(stream_key, axis), (), 0, length) for axis, length in enumerate(drawn.shape)]
    main_axis = drawn.shape.index(max(drawn.shape))
    beside = place[:main_axis] + [(place[main_axis] + 1) % drawn.shape[main_axis]] + place[main_axis + 1:]
    return drawn.at[tuple(place)].set(smallest).at[tuple(beside)].set(high)


def block_scale(own_key, extent, shards, least, largest):
    loudness, own = 1.0, jax.random.fold_in(own_key, 6)
    for axis_at, shards_of in shards:
        draws = jnp.exp(jax.random.uniform(jax.random.fold_in(own, axis_at), (shards_of,), jnp.float32, least / len(shards), largest / len(shards)))
        loudness = loudness * jnp.repeat(draws, extent[axis_at] // shards_of).reshape([-1 if axis == axis_at else 1 for axis in range(len(extent))])
    return loudness


def noise(own_key, dims, deviation, limit, pieces=(), kind=jnp.bfloat16):
    values = deviation * jax.random.normal(own_key, dims, jnp.float32)
    if pieces:
        values = values * block_scale(own_key, dims, pieces, -0.22, 0.18)
    return jnp.clip(values, -limit, limit).astype(kind)


def setup_inputs(seed: int = 0) -> dict:
    streams_of = jax.random.split(jax.random.key(seed), 9)
    features = noise(streams_of[0], (NODES, F), 1.0, 6.0, ((0, 32),), jnp.float32)
    tile_rows = with_ends(jax.random.randint(streams_of[1], (DEVICES * TILES_DEV,), 0, RB), jax.random.fold_in(streams_of[1], 1), 0, RB - 1).astype(jnp.int32)
    tile_cols = with_ends(jax.random.randint(streams_of[2], (DEVICES * TILES_DEV,), 0, POOL), jax.random.fold_in(streams_of[2], 1), 0, POOL - 1).astype(jnp.int32)
    tile_vals = noise(streams_of[3], (DEVICES * TILES_DEV, TILE, TILE), (TILE * 6) ** -0.5, 0.21875, ((0, 32),), jnp.float32)
    tile_count = draw_tile_count(jax.random.fold_in(streams_of[8], 71), 0)
    near_send = with_ends(jax.random.randint(streams_of[5], (DEVICES, N_DEV, CAP), 0, RB), jax.random.fold_in(streams_of[5], 1), 0, RB - 1).astype(jnp.int32)
    far_send = with_ends(jax.random.randint(streams_of[6], (DEVICES, 2, HCAP), 0, RB), jax.random.fold_in(streams_of[6], 1), 0, RB - 1).astype(jnp.int32)
    skew_raw = noise(streams_of[7], (L, F, F), F ** -0.5, 0.25, (), jnp.float32)
    return {"features": features, "tile_rows": tile_rows, "tile_cols": tile_cols, "tile_vals": tile_vals, "tile_count": tile_count, "near_send": near_send, "far_send": far_send, "skew_raw": skew_raw}


def pool_table(near_send, far_send):
    devices = N_DOM * N_DEV
    dev_ids = jnp.arange(devices, dtype=jnp.int32)
    part_ids = dev_ids // N_DEV
    local_ids = dev_ids % N_DEV
    own_ids = dev_ids[:, None] * RB + jnp.arange(RB, dtype=jnp.int32)[None, :]
    near_src = part_ids[:, None] * N_DEV + jnp.arange(N_DEV, dtype=jnp.int32)[None, :]
    near_ids = near_send[near_src, local_ids[:, None], :] + near_src[:, :, None] * RB
    near_ids = near_ids.reshape(devices, N_DEV * CAP)
    lower_src = ((part_ids - 1) % N_DOM) * N_DEV + local_ids
    upper_src = ((part_ids + 1) % N_DOM) * N_DEV + local_ids
    lower_ids = far_send[lower_src, 0, :] + lower_src[:, None] * RB
    upper_ids = far_send[upper_src, 1, :] + upper_src[:, None] * RB
    return jnp.concatenate([own_ids, near_ids, lower_ids, upper_ids], axis=1).astype(jnp.int32)


def adjacency(field, tile_rows, global_cols, tile_vals, live_mask):
    blocks = field.reshape(-1, TILE, field.shape[1])
    devices = N_DOM * N_DEV

    def one_device(index):
        col_ids = lax.dynamic_index_in_dim(global_cols, index, 0, keepdims=False)
        row_ids = lax.dynamic_index_in_dim(tile_rows, index, 0, keepdims=False)
        tile_part = lax.dynamic_index_in_dim(tile_vals, index, 0, keepdims=False)
        live = lax.dynamic_index_in_dim(live_mask, index, 0, keepdims=False)
        gathered = blocks[col_ids]
        product = jnp.einsum("tab,tbf->taf", tile_part, gathered, precision=lax.Precision.HIGHEST)
        product = product * live[:, None, None]
        summed = jnp.zeros((RB, TILE, field.shape[1]), jnp.float32)
        return summed.at[row_ids].add(product)

    result = lax.map(one_device, jnp.arange(devices, dtype=jnp.int32))
    return result.reshape(field.shape)


def reference(features, tile_rows, tile_cols, tile_vals, tile_count, near_send, far_send, skew_raw):
    devices = N_DOM * N_DEV
    table = pool_table(near_send, far_send)
    local_cols = tile_cols.reshape(devices, TILES_DEV)
    global_cols = jnp.take_along_axis(table, local_cols, axis=1).astype(jnp.int32)
    rows_dev = tile_rows.reshape(devices, TILES_DEV)
    vals_dev = tile_vals.reshape(devices, TILES_DEV, TILE, TILE)
    live_mask = (jnp.arange(TILES_DEV, dtype=jnp.int32)[None, :] < tile_count[:, None]).astype(jnp.float32)
    current = features
    for layer in range(L):
        skew = 0.5 * (skew_raw[layer] - skew_raw[layer].T)
        first = jnp.dot(adjacency(current, rows_dev, global_cols, vals_dev, live_mask), skew,
                        precision=lax.Precision.HIGHEST, preferred_element_type=jnp.float32)
        second = 0.5 * jnp.dot(adjacency(first, rows_dev, global_cols, vals_dev, live_mask), skew,
                               precision=lax.Precision.HIGHEST, preferred_element_type=jnp.float32)
        mixed = current + first + second
        pairs = mixed.reshape(mixed.shape[0], mixed.shape[1] // 2, 2)
        low_half = jnp.minimum(pairs[:, :, 0], pairs[:, :, 1])
        high_half = jnp.maximum(pairs[:, :, 0], pairs[:, :, 1])
        current = jnp.stack([low_half, high_half], axis=-1).reshape(mixed.shape)
    return current
```

```python
import functools

import jax
import jax.numpy as jnp
from jax import lax
from jax.experimental import pallas as pl
from jax.experimental.pallas import tpu as pltpu
from jax.sharding import PartitionSpec as P

TILE = 128
VMEM_LIMIT = 60 * 1024 * 1024


def dense_kernel(rows_ref, cols_ref, count_ref, vals_ref, own_ref, near_ref, far_ref):
    outs = (own_ref, near_ref, far_ref)
    for ref in outs:
        ref[...] = jnp.zeros_like(ref)

    def add(t, carry):
        row, col = rows_ref[t], cols_ref[t]
        first = 0
        for ref in outs:
            width = ref.shape[1]

            @pl.when((col >= first) & (col < first + width))
            def _(ref=ref, first=first):
                ref[row, col - first] += vals_ref[t]

            first += width
        return carry

    lax.fori_loop(0, count_ref[0], add, 0)


def dense_adjacency(tile_rows, tile_cols, tile_count, tile_vals, row_blocks, near, far):
    widths = (row_blocks, near, far)
    pool = sum(widths)
    smem = pl.BlockSpec(memory_space=pltpu.SMEM)
    vmem = pl.BlockSpec(memory_space=pltpu.VMEM)
    return pl.pallas_call(
        dense_kernel,
        out_shape=[jax.ShapeDtypeStruct((row_blocks, w, TILE, TILE), jnp.float32) for w in widths],
        in_specs=[smem, smem, smem, vmem],
        out_specs=[vmem] * 3,
        compiler_params=pltpu.CompilerParams(vmem_limit_bytes=VMEM_LIMIT),
        cost_estimate=pl.CostEstimate(
            flops=0,
            bytes_accessed=4 * TILE * TILE * (tile_vals.shape[0] + row_blocks * pool),
            transcendentals=0,
        ),
    )(tile_rows, tile_cols, tile_count, tile_vals)


def pair_sort_kernel(x_ref, o_ref):
    x = x_ref[...]
    width = x.shape[1]
    even = lax.broadcasted_iota(jnp.int32, x.shape, 1) % 2 == 0
    after = pltpu.roll(x, width - 1, 1)
    before = pltpu.roll(x, 1, 1)
    o_ref[...] = jnp.where(even, jnp.minimum(x, after), jnp.maximum(x, before))


def pair_sort(x):
    rows, width = x.shape
    block = pl.BlockSpec((2 * TILE, width), lambda i: (i, 0))
    return pl.pallas_call(
        pair_sort_kernel,
        grid=(rows // (2 * TILE),),
        out_shape=jax.ShapeDtypeStruct(x.shape, x.dtype),
        in_specs=[block],
        out_specs=block,
        cost_estimate=pl.CostEstimate(flops=rows * width * 4, bytes_accessed=8 * rows * width, transcendentals=0),
    )(x)


def times(a, b):
    return jnp.dot(a, b, precision=lax.Precision.HIGH, preferred_element_type=jnp.float32)


def apply_tiles(dense, blocks):
    r, c = dense.shape[:2]
    d = dense.transpose(0, 2, 1, 3).reshape(r * TILE, c * TILE)
    return times(d, blocks)


def exchange(field, near_send, far_send):
    width = field.shape[1]
    blocks = field.reshape(-1, TILE, width)
    peers = lax.axis_size("dom")
    up = [(i, (i + 1) % peers) for i in range(peers)]
    down = [(j, i) for i, j in up]
    to_peers = blocks[near_send[0].reshape(-1)]
    near = lax.all_to_all(to_peers, "dev", split_axis=0, concat_axis=0, tiled=True)
    lower = lax.ppermute(blocks[far_send[0, 0]], "dom", up)
    upper = lax.ppermute(blocks[far_send[0, 1]], "dom", down)
    far = jnp.concatenate([lower, upper], axis=0)
    return near.reshape(-1, width), far.reshape(-1, width)


def local(features, tile_rows, tile_cols, tile_vals, tile_count, near_send, far_send, skew_raw):
    row_blocks = features.shape[0] // TILE
    near_slots = near_send.shape[1] * near_send.shape[2]
    far_slots = 2 * far_send.shape[2]
    own, near, far = dense_adjacency(tile_rows, tile_cols, tile_count, tile_vals, row_blocks, near_slots, far_slots)

    current = features
    for layer in range(skew_raw.shape[0]):
        skew = 0.5 * (skew_raw[layer] - skew_raw[layer].T)
        half_square = 0.5 * jnp.dot(
            skew, skew, precision=lax.Precision.HIGHEST, preferred_element_type=jnp.float32
        )
        near_x, far_x = exchange(current, near_send, far_send)
        once = apply_tiles(own, current) + apply_tiles(far, far_x)
        once = once + apply_tiles(near, near_x)
        near_y, far_y = exchange(once, near_send, far_send)
        twice = apply_tiles(own, once) + apply_tiles(far, far_y)
        base = current + times(once, skew) + times(twice, half_square)
        mixed = base + times(apply_tiles(near, near_y), half_square)
        current = pair_sort(mixed)
    return current


def solution(mesh):
    nodes = ("dom", "dev")
    in_specs = (
        P(nodes, None),
        P(nodes),
        P(nodes),
        P(nodes, None, None),
        P(nodes),
        P(nodes, None, None),
        P(nodes, None, None),
        P(),
    )
    return jax.shard_map(local, mesh=mesh, in_specs=in_specs, out_specs=P(nodes, None), check_vma=False)
```

```python
import functools

import jax
import jax.numpy as jnp
from jax import lax
from jax.experimental import pallas as pl
from jax.experimental.pallas import tpu as pltpu
from jax.sharding import PartitionSpec as P

TILE = 128
STEP = 2
MIB = 1024 * 1024
SMALL = pl.CostEstimate(flops=1, bytes_accessed=1, transcendentals=0)


def split(x):
    high = x.astype(jnp.bfloat16)
    return high, (x - high.astype(jnp.float32)).astype(jnp.bfloat16)


def dot3(a_high, a_low, b_high, b_low):
    dot = functools.partial(jnp.dot, preferred_element_type=jnp.float32)
    return dot(a_high, b_high) + (dot(a_high, b_low) + dot(a_low, b_high))


def smem():
    return pl.BlockSpec(memory_space=pltpu.SMEM)


def whole(shape):
    return pl.BlockSpec(shape, lambda i: (0,) * len(shape))


def of_layer(weight):
    array, layer = weight
    return pl.BlockSpec((None,) + array.shape[1:], lambda i: (layer, 0, 0))


def rows_of(shape):
    return pl.BlockSpec((STEP,) + shape[1:], lambda i: (i,) + (0,) * (len(shape) - 1))


def dense_kernel(rows_ref, cols_ref, count_ref, vals_ref, *refs):
    outs, total = refs[:-1], refs[-1]
    total[...] = jnp.zeros_like(total)

    def add(t, carry):
        total[rows_ref[t], cols_ref[t]] += vals_ref[t]
        return carry

    lax.fori_loop(0, count_ref[0], add, 0)

    def write(r, carry):
        first = 0
        for high_ref, low_ref in zip(outs[::2], outs[1::2]):
            for c in range(high_ref.shape[2] // TILE):
                high, low = split(total[r, first + c])
                high_ref[r, :, c * TILE : (c + 1) * TILE] = high
                low_ref[r, :, c * TILE : (c + 1) * TILE] = low
            first += high_ref.shape[2] // TILE
        return carry

    lax.fori_loop(0, total.shape[0], write, 0)


def dense_adjacency(tile_rows, places, tile_count, tile_vals, row_blocks, widths):
    vmem = pl.BlockSpec(memory_space=pltpu.VMEM)
    out_shape = []
    for w in widths:
        out_shape += [jax.ShapeDtypeStruct((row_blocks, TILE, w * TILE), jnp.bfloat16)] * 2
    flat = pl.pallas_call(
        dense_kernel,
        out_shape=out_shape,
        in_specs=[smem(), smem(), smem(), vmem],
        out_specs=[vmem] * len(out_shape),
        scratch_shapes=[pltpu.VMEM((row_blocks, sum(widths), TILE, TILE), jnp.float32)],
        compiler_params=pltpu.CompilerParams(vmem_limit_bytes=60 * MIB),
        cost_estimate=SMALL,
    )(tile_rows, places, tile_count, tile_vals)
    return [(flat[2 * g], flat[2 * g + 1]) for g in range(len(widths))]


def weights_kernel(raw_ref, *refs):
    raw = raw_ref[0]
    skew = 0.5 * (raw - raw.T)
    square = 0.5 * jnp.dot(
        skew, skew, precision=lax.Precision.HIGHEST, preferred_element_type=jnp.float32
    )
    for ref, part in zip(refs, split(skew) + split(square)):
        ref[0] = part


def weights(skew_raw):
    block = pl.BlockSpec((1,) + skew_raw.shape[1:], lambda i: (i, 0, 0))
    return pl.pallas_call(
        weights_kernel,
        grid=(skew_raw.shape[0],),
        out_shape=[jax.ShapeDtypeStruct(skew_raw.shape, jnp.bfloat16)] * 4,
        in_specs=[block],
        out_specs=[block] * 4,
        compiler_params=pltpu.CompilerParams(vmem_limit_bytes=40 * MIB),
        cost_estimate=SMALL,
    )(skew_raw)


def load_split(x_refs, high, low):
    at = 0
    for x_ref in x_refs:
        for b in range(x_ref.shape[0]):
            high[at : at + TILE, :], low[at : at + TILE, :] = split(x_ref[b])
            at += TILE


def flat_rows(ref):
    return ref[...].reshape(-1, ref.shape[-1])


def load_product(x_refs, square_refs, high, low):
    load_split(x_refs, high, low)
    if square_refs:
        product = dot3(high[...], low[...], square_refs[0][...], square_refs[1][...])
        high[...], low[...] = split(product)


def apply_kernel(n_x, has_acc, squared, ah_ref, al_ref, *refs):
    x_refs = refs[:n_x]
    acc_ref = refs[n_x] if has_acc else None
    square_refs = refs[-5:-3] if squared else ()
    o_ref, high, low = refs[-3:]

    @pl.when(pl.program_id(0) == 0)
    def _():
        load_product(x_refs, square_refs, high, low)

    out = dot3(flat_rows(ah_ref), flat_rows(al_ref), high[...], low[...])
    if has_acc:
        out = out + flat_rows(acc_ref)
    o_ref[...] = out.reshape(o_ref.shape)


def front(x, count):
    return whole((count,) + x.shape[1:])


def apply_dense(dense, xs, acc=None, square=()):
    ah, al = dense
    width = xs[0][0].shape[-1]
    out = jax.ShapeDtypeStruct((ah.shape[0], TILE, width), jnp.float32)
    depth = ah.shape[2]
    args = [ah, al] + [x for x, _ in xs]
    specs = [rows_of(ah.shape), rows_of(al.shape)] + [front(x, n) for x, n in xs]
    if acc is not None:
        args.append(acc)
        specs.append(rows_of(acc.shape))
    args += [q for q, _ in square]
    specs += [of_layer(q) for q in square]
    return pl.pallas_call(
        functools.partial(apply_kernel, len(xs), acc is not None, bool(square)),
        grid=(ah.shape[0] // STEP,),
        out_shape=out,
        in_specs=specs,
        out_specs=rows_of(out.shape),
        scratch_shapes=[pltpu.VMEM((depth, width), jnp.bfloat16)] * 2,
        compiler_params=pltpu.CompilerParams(vmem_limit_bytes=40 * MIB),
        cost_estimate=SMALL,
    )(*args)


def mix_kernel(x_ref, once_ref, twice_ref, sh_ref, sl_ref, qh_ref, ql_ref, o_ref):
    out = flat_rows(x_ref) + dot3(*split(flat_rows(once_ref)), sh_ref[...], sl_ref[...])
    out = out + dot3(*split(flat_rows(twice_ref)), qh_ref[...], ql_ref[...])
    o_ref[...] = out.reshape(o_ref.shape)


def mix(x, once, twice, skew, square):
    block = rows_of(x.shape)
    factors = [*skew, *square]
    width = x.shape[-1]
    return pl.pallas_call(
        mix_kernel,
        grid=(x.shape[0] // STEP,),
        out_shape=jax.ShapeDtypeStruct(x.shape, jnp.float32),
        in_specs=[block] * 3 + [of_layer(w) for w in factors],
        out_specs=block,
        compiler_params=pltpu.CompilerParams(vmem_limit_bytes=40 * MIB),
        cost_estimate=SMALL,
    )(x, once, twice, *[w for w, _ in factors])


def picked(plan, me, near_ref, far_ref):
    for entries in plan:
        blocks = []
        for kind, index in entries:
            if kind == "near":
                peer = me ^ index
                blocks += [near_ref[peer, i] for i in range(near_ref.shape[1])]
            else:
                blocks += [far_ref[index, i] for i in range(far_ref.shape[1])]
        yield blocks


def copy_out(plan, me_ref, near_ref, far_ref, source, send_refs, sems):
    copies = []
    for ref, blocks in zip(send_refs, picked(plan, me_ref[0], near_ref, far_ref)):
        for i, block in enumerate(blocks):
            copies.append(pltpu.make_async_copy(source.at[block], ref.at[i], sems.at[len(copies)]))
            copies[-1].start()
    for copy in copies:
        copy.wait()


def plan_sizes(plan, near, far):
    return [sum(near.shape[1] if kind == "near" else far.shape[1] for kind, _ in e) for e in plan]


def pick_kernel(plan, me_ref, near_ref, far_ref, x_ref, *refs):
    copy_out(plan, me_ref, near_ref, far_ref, x_ref, refs[:-1], refs[-1])


def pick(x, route):
    plan, me, near, far = route
    sizes = plan_sizes(plan, near, far)
    hbm = pl.BlockSpec(memory_space=pl.ANY)
    return pl.pallas_call(
        functools.partial(pick_kernel, plan),
        out_shape=[jax.ShapeDtypeStruct((n,) + x.shape[1:], x.dtype) for n in sizes],
        in_specs=[smem()] * 3 + [pl.BlockSpec(memory_space=pltpu.VMEM)],
        out_specs=[hbm] * len(sizes),
        scratch_shapes=[pltpu.SemaphoreType.DMA((sum(sizes),))],
        compiler_params=pltpu.CompilerParams(vmem_limit_bytes=16 * MIB),
        cost_estimate=SMALL,
    )(me, near, far, x)


def finish_kernel(plan, n_x, squared, n_send, me_ref, near_ref, far_ref, ah_ref, al_ref, acc_ref, *refs):
    refs = list(refs)
    x_refs = [refs.pop(0) for _ in range(n_x)]
    square_refs = [refs.pop(0) for _ in range(2 * squared)]
    o_ref = refs.pop(0)
    send_refs = [refs.pop(0) for _ in range(n_send)]
    high, low = refs.pop(0), refs.pop(0)
    step = pl.program_id(0)

    @pl.when(step == 0)
    def _():
        load_product(x_refs, square_refs, high, low)

    out = dot3(flat_rows(ah_ref), flat_rows(al_ref), high[...], low[...]) + flat_rows(acc_ref)
    if squared:
        width = out.shape[1]
        even = lax.broadcasted_iota(jnp.int32, out.shape, 1) % 2 == 0
        after, before = pltpu.roll(out, width - 1, 1), pltpu.roll(out, 1, 1)
        out = jnp.where(even, jnp.minimum(out, after), jnp.maximum(out, before))
    out = out.reshape(o_ref.shape)
    o_ref[...] = out
    if n_send:
        kept, sems = refs
        kept[pl.ds(step * STEP, STEP)] = out

        @pl.when(step == pl.num_programs(0) - 1)
        def _():
            copy_out(plan, me_ref, near_ref, far_ref, kept, send_refs, sems)


def finish(dense, xs, acc, route, square=(), send=True):
    plan, me, near, far = route
    sizes = plan_sizes(plan, near, far) if send else []
    ah, al = dense
    depth, width = ah.shape[2], acc.shape[2]
    field = jax.ShapeDtypeStruct(acc.shape, jnp.float32)
    args = [me, near, far, ah, al, acc] + [x for x, _ in xs]
    specs = [smem()] * 3 + [rows_of(ah.shape), rows_of(al.shape), rows_of(acc.shape)]
    specs += [front(x, n) for x, n in xs]
    args += [q for q, _ in square]
    specs += [of_layer(q) for q in square]
    scratch = [pltpu.VMEM((depth, width), jnp.bfloat16)] * 2
    if send:
        scratch += [pltpu.VMEM(acc.shape, jnp.float32), pltpu.SemaphoreType.DMA((sum(sizes),))]
    return pl.pallas_call(
        functools.partial(finish_kernel, plan, len(xs), bool(square), len(sizes)),
        grid=(acc.shape[0] // STEP,),
        out_shape=[field] + [jax.ShapeDtypeStruct((n, TILE, width), jnp.float32) for n in sizes],
        in_specs=specs,
        out_specs=[rows_of(acc.shape)] + [pl.BlockSpec(memory_space=pl.ANY)] * len(sizes),
        scratch_shapes=scratch,
        compiler_params=pltpu.CompilerParams(vmem_limit_bytes=40 * MIB),
        cost_estimate=SMALL,
    )(*args)


def tie(values, *others):
    done = lax.optimization_barrier(tuple(values) + tuple(others))
    return list(done[: len(values)]), list(done[len(values) :])


def local(features, tile_rows, tile_cols, tile_vals, tile_count, near_send, far_send, skew_raw):
    width = features.shape[1]
    row_blocks = features.shape[0] // TILE
    peers, cap, hcap = near_send.shape[1], near_send.shape[2], far_send.shape[2]
    domains = lax.axis_size("dom")
    d = lax.axis_index("dev")
    me = d.astype(jnp.int32).reshape(1)

    chips = list(range(1, peers // 2))[::-1]
    plan = tuple(
        [(("near", 2 * j), ("near", 2 * j + 1)) for j in chips]
        + [(("far", 0),), (("far", 1),), (("near", 1),)]
    )
    route = (plan, me, near_send[0], far_send[0])

    widths = (row_blocks, 2 * hcap + cap * len(chips), cap * (1 + len(chips)))
    place_of = [0] * peers
    for at, j in enumerate(chips):
        place_of[2 * j] = row_blocks + 2 * hcap + at * cap
    for at, j in enumerate([0] + chips):
        place_of[2 * j + 1] = row_blocks + widths[1] + at * cap
    slot = tile_cols
    near_at = slot - row_blocks
    source, item = near_at // cap, near_at % cap
    source_safe = jnp.clip(source, 0, peers - 1)
    near_place = jnp.take(jnp.array(place_of, jnp.int32), source_safe ^ d) + item
    self_place = jnp.take(near_send[0].reshape(-1), d * cap + item)
    near_place = jnp.where(source_safe == d, self_place, near_place)
    far_place = slot - row_blocks - peers * cap + row_blocks
    places = jnp.where(
        slot < row_blocks, slot, jnp.where(slot < row_blocks + peers * cap, near_place, far_place)
    ).astype(jnp.int32)

    own_a, direct_a, core_a = dense_adjacency(tile_rows, places, tile_count, tile_vals, row_blocks, widths)

    def swap(x, k):
        return lax.ppermute(x, "dev", [(i, i ^ k) for i in range(peers)])

    up = [(i, (i + 1) % domains) for i in range(domains)]
    down = [(j, i) for i, j in up]

    def start(sends):
        n = len(chips)
        near = [swap(s, 2 * j) for s, j in zip(sends[:n], chips)]
        lower = lax.ppermute(sends[n], "dom", up)
        upper = lax.ppermute(sends[n + 1], "dom", down)
        return near, lower, upper, sends[n + 2]

    def arrive(flight, acc, square=()):
        near, lower, upper, to_core = flight
        near, (lower, upper, to_core, acc) = tie(near, lower, upper, to_core, acc)
        passed = swap(jnp.concatenate([to_core] + [r[cap:] for r in near], axis=0), 1)
        direct = [(lower, hcap), (upper, hcap)] + [(r, cap) for r in near]
        return apply_dense(direct_a, direct, acc, square), [(passed, passed.shape[0])]

    current = features.reshape(row_blocks, TILE, width)
    sends = pick(current, route)
    parts = weights(skew_raw)
    layers = skew_raw.shape[0]
    for layer in range(layers):
        flight = start(sends)
        skew, square = [(w, layer) for w in parts[:2]], [(w, layer) for w in parts[2:]]
        acc, passed = arrive(flight, apply_dense(own_a, [(current, row_blocks)]))
        once, *sends = finish(core_a, passed, acc, route)
        flight = start(sends)
        base = mix(current, once, apply_dense(own_a, [(once, row_blocks)]), skew, square)
        base, passed = arrive(flight, base, square)
        current, *sends = finish(core_a, passed, base, route, square, layer < layers - 1)
    return current.reshape(features.shape)


def solution(mesh):
    nodes = ("dom", "dev")
    in_specs = (
        P(nodes, None),
        P(nodes),
        P(nodes),
        P(nodes, None, None),
        P(nodes),
        P(nodes, None, None),
        P(nodes, None, None),
        P(),
    )
    return jax.shard_map(local, mesh=mesh, in_specs=in_specs, out_specs=P(nodes, None), check_vma=False)
```

```python
import functools

import jax
import jax.numpy as jnp
from jax import lax
from jax.experimental import pallas as pl
from jax.experimental.pallas import tpu as pltpu
from jax.sharding import PartitionSpec as P

TILE = 128
STEP = 2
MIB = 1024 * 1024
SMALL = pl.CostEstimate(flops=1, bytes_accessed=1, transcendentals=0)


def split(x):
    high = x.astype(jnp.bfloat16)
    return high, (x - high.astype(jnp.float32)).astype(jnp.bfloat16)


def dot3(a_high, a_low, b_high, b_low):
    dot = functools.partial(jnp.dot, preferred_element_type=jnp.float32)
    return dot(a_high, b_high) + (dot(a_high, b_low) + dot(a_low, b_high))


def smem():
    return pl.BlockSpec(memory_space=pltpu.SMEM)


def whole(shape):
    return pl.BlockSpec(shape, lambda i: (0,) * len(shape))


def of_layer(weight):
    array, layer = weight
    return pl.BlockSpec((None,) + array.shape[1:], lambda i: (layer, 0, 0))


def rows_of(shape):
    return pl.BlockSpec((STEP,) + shape[1:], lambda i: (i,) + (0,) * (len(shape) - 1))


def dense_kernel(rows_ref, cols_ref, count_ref, vals_ref, *refs):
    outs, total = refs[:-1], refs[-1]
    total[...] = jnp.zeros_like(total)

    def add(t, carry):
        total[rows_ref[t], cols_ref[t]] += vals_ref[t]
        return carry

    lax.fori_loop(0, count_ref[0], add, 0)

    def write(r, carry):
        first = 0
        for high_ref, low_ref in zip(outs[::2], outs[1::2]):
            for c in range(high_ref.shape[2] // TILE):
                high, low = split(total[r, first + c])
                high_ref[r, :, c * TILE : (c + 1) * TILE] = high
                low_ref[r, :, c * TILE : (c + 1) * TILE] = low
            first += high_ref.shape[2] // TILE
        return carry

    lax.fori_loop(0, total.shape[0], write, 0)


def dense_adjacency(tile_rows, places, tile_count, tile_vals, row_blocks, widths):
    vmem = pl.BlockSpec(memory_space=pltpu.VMEM)
    out_shape = []
    for w in widths:
        out_shape += [jax.ShapeDtypeStruct((row_blocks, TILE, w * TILE), jnp.bfloat16)] * 2
    need = 4 * TILE * TILE * (tile_vals.shape[0] + 2 * row_blocks * sum(widths))
    flat = pl.pallas_call(
        dense_kernel,
        out_shape=out_shape,
        in_specs=[smem(), smem(), smem(), vmem],
        out_specs=[vmem] * len(out_shape),
        scratch_shapes=[pltpu.VMEM((row_blocks, sum(widths), TILE, TILE), jnp.float32)],
        compiler_params=pltpu.CompilerParams(vmem_limit_bytes=need + 4 * MIB),
        cost_estimate=SMALL,
    )(tile_rows, places, tile_count, tile_vals)
    return [(flat[2 * g], flat[2 * g + 1]) for g in range(len(widths))]


def weights_kernel(raw_ref, *refs):
    raw = raw_ref[0]
    skew = 0.5 * (raw - raw.T)
    square = 0.5 * jnp.dot(
        skew, skew, precision=lax.Precision.HIGHEST, preferred_element_type=jnp.float32
    )
    for ref, part in zip(refs, split(skew) + split(square)):
        ref[0] = part


def weights(skew_raw):
    block = pl.BlockSpec((1,) + skew_raw.shape[1:], lambda i: (i, 0, 0))
    return pl.pallas_call(
        weights_kernel,
        grid=(skew_raw.shape[0],),
        out_shape=[jax.ShapeDtypeStruct(skew_raw.shape, jnp.bfloat16)] * 4,
        in_specs=[block],
        out_specs=[block] * 4,
        compiler_params=pltpu.CompilerParams(vmem_limit_bytes=24 * MIB),
        cost_estimate=SMALL,
    )(skew_raw)


def load_split(x_refs, high, low):
    at = 0
    for x_ref in x_refs:
        for b in range(x_ref.shape[0]):
            high[at : at + TILE, :], low[at : at + TILE, :] = split(x_ref[b])
            at += TILE


def flat_rows(ref):
    return ref[...].reshape(-1, ref.shape[-1])


def load_product(x_refs, square_refs, high, low):
    load_split(x_refs, high, low)
    if square_refs:
        product = dot3(high[...], low[...], square_refs[0][...], square_refs[1][...])
        high[...], low[...] = split(product)


def apply_kernel(n_x, has_acc, squared, ah_ref, al_ref, *refs):
    x_refs = refs[:n_x]
    acc_ref = refs[n_x] if has_acc else None
    square_refs = refs[-5:-3] if squared else ()
    o_ref, high, low = refs[-3:]

    @pl.when(pl.program_id(0) == 0)
    def _():
        load_product(x_refs, square_refs, high, low)

    out = dot3(flat_rows(ah_ref), flat_rows(al_ref), high[...], low[...])
    if has_acc:
        out = out + flat_rows(acc_ref)
    o_ref[...] = out.reshape(o_ref.shape)


def front(x, count):
    return whole((count,) + x.shape[1:])


def apply_dense(dense, xs, acc=None, square=()):
    ah, al = dense
    width = xs[0][0].shape[-1]
    out = jax.ShapeDtypeStruct((ah.shape[0], TILE, width), jnp.float32)
    depth = ah.shape[2]
    args = [ah, al] + [x for x, _ in xs]
    specs = [rows_of(ah.shape), rows_of(al.shape)] + [front(x, n) for x, n in xs]
    if acc is not None:
        args.append(acc)
        specs.append(rows_of(acc.shape))
    args += [q for q, _ in square]
    specs += [of_layer(q) for q in square]
    return pl.pallas_call(
        functools.partial(apply_kernel, len(xs), acc is not None, bool(square)),
        grid=(ah.shape[0] // STEP,),
        out_shape=out,
        in_specs=specs,
        out_specs=rows_of(out.shape),
        scratch_shapes=[pltpu.VMEM((depth, width), jnp.bfloat16)] * 2,
        compiler_params=pltpu.CompilerParams(vmem_limit_bytes=24 * MIB),
        cost_estimate=SMALL,
    )(*args)


def mix_kernel(x_ref, once_ref, twice_ref, sh_ref, sl_ref, qh_ref, ql_ref, o_ref):
    out = flat_rows(x_ref) + dot3(*split(flat_rows(once_ref)), sh_ref[...], sl_ref[...])
    out = out + dot3(*split(flat_rows(twice_ref)), qh_ref[...], ql_ref[...])
    o_ref[...] = out.reshape(o_ref.shape)


def mix(x, once, twice, skew, square):
    block = rows_of(x.shape)
    factors = [*skew, *square]
    width = x.shape[-1]
    return pl.pallas_call(
        mix_kernel,
        grid=(x.shape[0] // STEP,),
        out_shape=jax.ShapeDtypeStruct(x.shape, jnp.float32),
        in_specs=[block] * 3 + [of_layer(w) for w in factors],
        out_specs=block,
        compiler_params=pltpu.CompilerParams(vmem_limit_bytes=24 * MIB),
        cost_estimate=SMALL,
    )(x, once, twice, *[w for w, _ in factors])


def picked(plan, me, near_ref, far_ref):
    for entries in plan:
        blocks = []
        for kind, index in entries:
            if kind == "near":
                peer = me ^ index
                blocks += [near_ref[peer, i] for i in range(near_ref.shape[1])]
            else:
                blocks += [far_ref[index, i] for i in range(far_ref.shape[1])]
        yield blocks


def copy_out(plan, me_ref, near_ref, far_ref, source, send_refs, sems):
    copies = []
    for ref, blocks in zip(send_refs, picked(plan, me_ref[0], near_ref, far_ref)):
        for i, block in enumerate(blocks):
            copies.append(pltpu.make_async_copy(source.at[block], ref.at[i], sems.at[len(copies)]))
            copies[-1].start()
    for copy in copies:
        copy.wait()


def plan_sizes(plan, near, far):
    return [sum(near.shape[1] if kind == "near" else far.shape[1] for kind, _ in e) for e in plan]


def pick_kernel(plan, me_ref, near_ref, far_ref, x_ref, *refs):
    copy_out(plan, me_ref, near_ref, far_ref, x_ref, refs[:-1], refs[-1])


def pick(x, route):
    plan, me, near, far = route
    sizes = plan_sizes(plan, near, far)
    hbm = pl.BlockSpec(memory_space=pl.ANY)
    return pl.pallas_call(
        functools.partial(pick_kernel, plan),
        out_shape=[jax.ShapeDtypeStruct((n,) + x.shape[1:], x.dtype) for n in sizes],
        in_specs=[smem()] * 3 + [pl.BlockSpec(memory_space=pltpu.VMEM)],
        out_specs=[hbm] * len(sizes),
        scratch_shapes=[pltpu.SemaphoreType.DMA((sum(sizes),))],
        compiler_params=pltpu.CompilerParams(vmem_limit_bytes=16 * MIB),
        cost_estimate=SMALL,
    )(me, near, far, x)


def finish_kernel(plan, n_x, squared, n_send, me_ref, near_ref, far_ref, ah_ref, al_ref, acc_ref, *refs):
    refs = list(refs)
    x_refs = [refs.pop(0) for _ in range(n_x)]
    square_refs = [refs.pop(0) for _ in range(2 * squared)]
    o_ref = refs.pop(0)
    send_refs = [refs.pop(0) for _ in range(n_send)]
    high, low = refs.pop(0), refs.pop(0)
    step = pl.program_id(0)

    @pl.when(step == 0)
    def _():
        load_product(x_refs, square_refs, high, low)

    out = dot3(flat_rows(ah_ref), flat_rows(al_ref), high[...], low[...]) + flat_rows(acc_ref)
    if squared:
        width = out.shape[1]
        even = lax.broadcasted_iota(jnp.int32, out.shape, 1) % 2 == 0
        after, before = pltpu.roll(out, width - 1, 1), pltpu.roll(out, 1, 1)
        out = jnp.where(even, jnp.minimum(out, after), jnp.maximum(out, before))
    out = out.reshape(o_ref.shape)
    o_ref[...] = out
    if n_send:
        kept, sems = refs
        kept[pl.ds(step * STEP, STEP)] = out

        @pl.when(step == pl.num_programs(0) - 1)
        def _():
            copy_out(plan, me_ref, near_ref, far_ref, kept, send_refs, sems)


def finish(dense, xs, acc, route, square=(), send=True):
    plan, me, near, far = route
    sizes = plan_sizes(plan, near, far) if send else []
    ah, al = dense
    depth, width = ah.shape[2], acc.shape[2]
    field = jax.ShapeDtypeStruct(acc.shape, jnp.float32)
    args = [me, near, far, ah, al, acc] + [x for x, _ in xs]
    specs = [smem()] * 3 + [rows_of(ah.shape), rows_of(al.shape), rows_of(acc.shape)]
    specs += [front(x, n) for x, n in xs]
    args += [q for q, _ in square]
    specs += [of_layer(q) for q in square]
    scratch = [pltpu.VMEM((depth, width), jnp.bfloat16)] * 2
    if send:
        scratch += [pltpu.VMEM(acc.shape, jnp.float32), pltpu.SemaphoreType.DMA((sum(sizes),))]
    return pl.pallas_call(
        functools.partial(finish_kernel, plan, len(xs), bool(square), len(sizes)),
        grid=(acc.shape[0] // STEP,),
        out_shape=[field] + [jax.ShapeDtypeStruct((n, TILE, width), jnp.float32) for n in sizes],
        in_specs=specs,
        out_specs=[rows_of(acc.shape)] + [pl.BlockSpec(memory_space=pl.ANY)] * len(sizes),
        scratch_shapes=scratch,
        compiler_params=pltpu.CompilerParams(vmem_limit_bytes=24 * MIB),
        cost_estimate=SMALL,
    )(*args)


def tie(values, *others):
    done = lax.optimization_barrier(tuple(values) + tuple(others))
    return list(done[: len(values)]), list(done[len(values) :])


def local(features, tile_rows, tile_cols, tile_vals, tile_count, near_send, far_send, skew_raw):
    width = features.shape[1]
    row_blocks = features.shape[0] // TILE
    peers, cap, hcap = near_send.shape[1], near_send.shape[2], far_send.shape[2]
    domains = lax.axis_size("dom")
    d = lax.axis_index("dev")
    me = d.astype(jnp.int32).reshape(1)

    late = list(range(peers // 4, peers // 2))[::-1]
    early = list(range(1, peers // 4))
    plan = tuple(
        [(("near", 2 * j), ("near", 2 * j + 1)) for j in late + early]
        + [(("far", 0),), (("far", 1),), (("near", 1),)]
    )
    route = (plan, me, near_send[0], far_send[0])

    early_k = [2 * j for j in early] + [1] + [2 * j + 1 for j in early]
    late_k = [2 * j for j in late] + [2 * j + 1 for j in late]
    widths = (row_blocks, 2 * hcap + cap * len(early_k), cap * len(late_k))
    place_of = [0] * peers
    for at, k in enumerate(early_k):
        place_of[k] = row_blocks + 2 * hcap + at * cap
    for at, k in enumerate(late_k):
        place_of[k] = row_blocks + widths[1] + at * cap
    slot = tile_cols
    near_at = slot - row_blocks
    source, item = near_at // cap, near_at % cap
    source_safe = jnp.clip(source, 0, peers - 1)
    near_place = jnp.take(jnp.array(place_of, jnp.int32), source_safe ^ d) + item
    self_place = jnp.take(near_send[0].reshape(-1), d * cap + item)
    near_place = jnp.where(source_safe == d, self_place, near_place)
    far_place = slot - row_blocks - peers * cap + row_blocks
    places = jnp.where(
        slot < row_blocks, slot, jnp.where(slot < row_blocks + peers * cap, near_place, far_place)
    ).astype(jnp.int32)

    own_a, early_a, late_a = dense_adjacency(tile_rows, places, tile_count, tile_vals, row_blocks, widths)

    def swap(x, k):
        return lax.ppermute(x, "dev", [(i, i ^ k) for i in range(peers)])

    up = [(i, (i + 1) % domains) for i in range(domains)]
    down = [(j, i) for i, j in up]

    def start(sends):
        chips = late + early
        near = [swap(s, 2 * j) for s, j in zip(sends, chips)]
        lower = lax.ppermute(sends[len(chips)], "dom", up)
        upper = lax.ppermute(sends[len(chips) + 1], "dom", down)
        return near[: len(late)], near[len(late) :], lower, upper, sends[-1]

    def arrive(flight, acc, square=()):
        long, short, lower, upper, to_core = flight
        (to_core, *short), (lower, upper, acc) = tie([to_core] + short, lower, upper, acc)
        across = [swap(to_core, 1)] + [swap(r[cap:], 1) for r in short]
        arrived = [(lower, hcap), (upper, hcap)] + [(r, cap) for r in short + across]
        acc = apply_dense(early_a, arrived, acc, square)
        long, (acc,) = tie(long, acc)
        passed = swap(jnp.concatenate([r[cap:] for r in long], axis=0), 1)
        return acc, [(r, cap) for r in long] + [(passed, passed.shape[0])]

    current = features.reshape(row_blocks, TILE, width)
    sends = pick(current, route)
    parts = weights(skew_raw)
    layers = skew_raw.shape[0]
    for layer in range(layers):
        flight = start(sends)
        skew, square = [(w, layer) for w in parts[:2]], [(w, layer) for w in parts[2:]]
        acc, arrived = arrive(flight, apply_dense(own_a, [(current, row_blocks)]))
        once, *sends = finish(late_a, arrived, acc, route)
        flight = start(sends)
        base = mix(current, once, apply_dense(own_a, [(once, row_blocks)]), skew, square)
        base, arrived = arrive(flight, base, square)
        current, *sends = finish(late_a, arrived, base, route, square, layer < layers - 1)
    return current.reshape(features.shape)


def solution(mesh):
    nodes = ("dom", "dev")
    in_specs = (
        P(nodes, None),
        P(nodes),
        P(nodes),
        P(nodes, None, None),
        P(nodes),
        P(nodes, None, None),
        P(nodes, None, None),
        P(),
    )
    return jax.shard_map(local, mesh=mesh, in_specs=in_specs, out_specs=P(nodes, None), check_vma=False)
```

```python
import functools

import jax
import jax.numpy as jnp
from jax import lax
from jax.experimental import pallas as pl
from jax.experimental.pallas import tpu as pltpu
from jax.sharding import PartitionSpec as P

TILE = 128
STEP = 2
MIB = 1024 * 1024
SMALL = pl.CostEstimate(flops=1, bytes_accessed=1, transcendentals=0)


def split(x):
    high = x.astype(jnp.bfloat16)
    return high, (x - high.astype(jnp.float32)).astype(jnp.bfloat16)


def dot3(a_high, a_low, b_high, b_low):
    dot = functools.partial(jnp.dot, preferred_element_type=jnp.float32)
    return dot(a_high, b_high) + (dot(a_high, b_low) + dot(a_low, b_high))


def smem():
    return pl.BlockSpec(memory_space=pltpu.SMEM)


def whole(shape):
    return pl.BlockSpec(shape, lambda i: (0,) * len(shape))


def of_layer(weight):
    array, layer = weight
    return pl.BlockSpec((None,) + array.shape[1:], lambda i: (layer, 0, 0))


def rows_of(shape):
    return pl.BlockSpec((STEP,) + shape[1:], lambda i: (i,) + (0,) * (len(shape) - 1))


def dense_kernel(rows_ref, cols_ref, count_ref, vals_ref, *refs):
    outs, total = refs[:-1], refs[-1]
    total[...] = jnp.zeros_like(total)

    def add(t, carry):
        total[rows_ref[t], cols_ref[t]] += vals_ref[t]
        return carry

    lax.fori_loop(0, count_ref[0], add, 0)

    def write(r, carry):
        first = 0
        for high_ref, low_ref in zip(outs[::2], outs[1::2]):
            for c in range(high_ref.shape[2] // TILE):
                high, low = split(total[r, first + c])
                high_ref[r, :, c * TILE : (c + 1) * TILE] = high
                low_ref[r, :, c * TILE : (c + 1) * TILE] = low
            first += high_ref.shape[2] // TILE
        return carry

    lax.fori_loop(0, total.shape[0], write, 0)


def dense_adjacency(tile_rows, places, tile_count, tile_vals, row_blocks, widths):
    vmem = pl.BlockSpec(memory_space=pltpu.VMEM)
    out_shape = []
    for w in widths:
        out_shape += [jax.ShapeDtypeStruct((row_blocks, TILE, w * TILE), jnp.bfloat16)] * 2
    need = 4 * TILE * TILE * (tile_vals.shape[0] + 2 * row_blocks * sum(widths))
    flat = pl.pallas_call(
        dense_kernel,
        out_shape=out_shape,
        in_specs=[smem(), smem(), smem(), vmem],
        out_specs=[vmem] * len(out_shape),
        scratch_shapes=[pltpu.VMEM((row_blocks, sum(widths), TILE, TILE), jnp.float32)],
        compiler_params=pltpu.CompilerParams(vmem_limit_bytes=need + 4 * MIB),
        cost_estimate=SMALL,
    )(tile_rows, places, tile_count, tile_vals)
    return [(flat[2 * g], flat[2 * g + 1]) for g in range(len(widths))]


def weights_kernel(raw_ref, *refs):
    raw = raw_ref[0]
    skew = 0.5 * (raw - raw.T)
    square = 0.5 * jnp.dot(
        skew, skew, precision=lax.Precision.HIGHEST, preferred_element_type=jnp.float32
    )
    for ref, part in zip(refs, split(skew) + split(square)):
        ref[0] = part


def weights(skew_raw):
    block = pl.BlockSpec((1,) + skew_raw.shape[1:], lambda i: (i, 0, 0))
    return pl.pallas_call(
        weights_kernel,
        grid=(skew_raw.shape[0],),
        out_shape=[jax.ShapeDtypeStruct(skew_raw.shape, jnp.bfloat16)] * 4,
        in_specs=[block],
        out_specs=[block] * 4,
        compiler_params=pltpu.CompilerParams(vmem_limit_bytes=24 * MIB),
        cost_estimate=SMALL,
    )(skew_raw)


def load_split(x_refs, high, low):
    at = 0
    for x_ref in x_refs:
        for b in range(x_ref.shape[0]):
            high[at : at + TILE, :], low[at : at + TILE, :] = split(x_ref[b])
            at += TILE


def flat_rows(ref):
    return ref[...].reshape(-1, ref.shape[-1])


def load_product(x_refs, square_refs, high, low):
    load_split(x_refs, high, low)
    if square_refs:
        product = dot3(high[...], low[...], square_refs[0][...], square_refs[1][...])
        high[...], low[...] = split(product)


def apply_kernel(n_x, has_acc, squared, ah_ref, al_ref, *refs):
    x_refs = refs[:n_x]
    acc_ref = refs[n_x] if has_acc else None
    square_refs = refs[-5:-3] if squared else ()
    o_ref, high, low = refs[-3:]

    @pl.when(pl.program_id(0) == 0)
    def _():
        load_product(x_refs, square_refs, high, low)

    out = dot3(flat_rows(ah_ref), flat_rows(al_ref), high[...], low[...])
    if has_acc:
        out = out + flat_rows(acc_ref)
    o_ref[...] = out.reshape(o_ref.shape)


def front(x, count):
    return whole((count,) + x.shape[1:])


def apply_dense(dense, xs, acc=None, square=()):
    ah, al = dense
    width = xs[0][0].shape[-1]
    out = jax.ShapeDtypeStruct((ah.shape[0], TILE, width), jnp.float32)
    depth = ah.shape[2]
    args = [ah, al] + [x for x, _ in xs]
    specs = [rows_of(ah.shape), rows_of(al.shape)] + [front(x, n) for x, n in xs]
    if acc is not None:
        args.append(acc)
        specs.append(rows_of(acc.shape))
    args += [q for q, _ in square]
    specs += [of_layer(q) for q in square]
    return pl.pallas_call(
        functools.partial(apply_kernel, len(xs), acc is not None, bool(square)),
        grid=(ah.shape[0] // STEP,),
        out_shape=out,
        in_specs=specs,
        out_specs=rows_of(out.shape),
        scratch_shapes=[pltpu.VMEM((depth, width), jnp.bfloat16)] * 2,
        compiler_params=pltpu.CompilerParams(vmem_limit_bytes=8 * MIB + 22 * depth * width),
        cost_estimate=SMALL,
    )(*args)


def mix_kernel(x_ref, once_ref, twice_ref, sh_ref, sl_ref, qh_ref, ql_ref, o_ref):
    out = flat_rows(x_ref) + dot3(*split(flat_rows(once_ref)), sh_ref[...], sl_ref[...])
    out = out + dot3(*split(flat_rows(twice_ref)), qh_ref[...], ql_ref[...])
    o_ref[...] = out.reshape(o_ref.shape)


def mix(x, once, twice, skew, square):
    block = rows_of(x.shape)
    factors = [*skew, *square]
    width = x.shape[-1]
    return pl.pallas_call(
        mix_kernel,
        grid=(x.shape[0] // STEP,),
        out_shape=jax.ShapeDtypeStruct(x.shape, jnp.float32),
        in_specs=[block] * 3 + [of_layer(w) for w in factors],
        out_specs=block,
        compiler_params=pltpu.CompilerParams(vmem_limit_bytes=24 * MIB),
        cost_estimate=SMALL,
    )(x, once, twice, *[w for w, _ in factors])


def picked(plan, me, near_ref, far_ref):
    for entries in plan:
        blocks = []
        for kind, index in entries:
            if kind == "near":
                peer = me ^ index
                blocks += [near_ref[peer, i] for i in range(near_ref.shape[1])]
            else:
                blocks += [far_ref[index, i] for i in range(far_ref.shape[1])]
        yield blocks


def copy_out(plan, me_ref, near_ref, far_ref, source, send_refs, sems):
    copies = []
    for ref, blocks in zip(send_refs, picked(plan, me_ref[0], near_ref, far_ref)):
        for i, block in enumerate(blocks):
            copies.append(pltpu.make_async_copy(source.at[block], ref.at[i], sems.at[len(copies)]))
            copies[-1].start()
    for copy in copies:
        copy.wait()


def plan_sizes(plan, near, far):
    return [sum(near.shape[1] if kind == "near" else far.shape[1] for kind, _ in e) for e in plan]


def pick_kernel(plan, me_ref, near_ref, far_ref, x_ref, *refs):
    copy_out(plan, me_ref, near_ref, far_ref, x_ref, refs[:-1], refs[-1])


def pick(x, route):
    plan, me, near, far = route
    sizes = plan_sizes(plan, near, far)
    hbm = pl.BlockSpec(memory_space=pl.ANY)
    return pl.pallas_call(
        functools.partial(pick_kernel, plan),
        out_shape=[jax.ShapeDtypeStruct((n,) + x.shape[1:], x.dtype) for n in sizes],
        in_specs=[smem()] * 3 + [pl.BlockSpec(memory_space=pltpu.VMEM)],
        out_specs=[hbm] * len(sizes),
        scratch_shapes=[pltpu.SemaphoreType.DMA((sum(sizes),))],
        compiler_params=pltpu.CompilerParams(vmem_limit_bytes=16 * MIB),
        cost_estimate=SMALL,
    )(me, near, far, x)


def finish_kernel(plan, n_x, squared, n_send, me_ref, near_ref, far_ref, ah_ref, al_ref, acc_ref, *refs):
    refs = list(refs)
    x_refs = [refs.pop(0) for _ in range(n_x)]
    square_refs = [refs.pop(0) for _ in range(2 * squared)]
    o_ref = refs.pop(0)
    send_refs = [refs.pop(0) for _ in range(n_send)]
    high, low = refs.pop(0), refs.pop(0)
    step = pl.program_id(0)

    @pl.when(step == 0)
    def _():
        load_product(x_refs, square_refs, high, low)

    out = dot3(flat_rows(ah_ref), flat_rows(al_ref), high[...], low[...]) + flat_rows(acc_ref)
    if squared:
        width = out.shape[1]
        even = lax.broadcasted_iota(jnp.int32, out.shape, 1) % 2 == 0
        after, before = pltpu.roll(out, width - 1, 1), pltpu.roll(out, 1, 1)
        out = jnp.where(even, jnp.minimum(out, after), jnp.maximum(out, before))
    out = out.reshape(o_ref.shape)
    o_ref[...] = out
    if n_send:
        kept, sems = refs
        kept[pl.ds(step * STEP, STEP)] = out

        @pl.when(step == pl.num_programs(0) - 1)
        def _():
            copy_out(plan, me_ref, near_ref, far_ref, kept, send_refs, sems)


def finish(dense, xs, acc, route, square=(), send=True):
    plan, me, near, far = route
    sizes = plan_sizes(plan, near, far) if send else []
    ah, al = dense
    depth, width = ah.shape[2], acc.shape[2]
    field = jax.ShapeDtypeStruct(acc.shape, jnp.float32)
    args = [me, near, far, ah, al, acc] + [x for x, _ in xs]
    specs = [smem()] * 3 + [rows_of(ah.shape), rows_of(al.shape), rows_of(acc.shape)]
    specs += [front(x, n) for x, n in xs]
    args += [q for q, _ in square]
    specs += [of_layer(q) for q in square]
    scratch = [pltpu.VMEM((depth, width), jnp.bfloat16)] * 2
    if send:
        scratch += [pltpu.VMEM(acc.shape, jnp.float32), pltpu.SemaphoreType.DMA((sum(sizes),))]
    return pl.pallas_call(
        functools.partial(finish_kernel, plan, len(xs), bool(square), len(sizes)),
        grid=(acc.shape[0] // STEP,),
        out_shape=[field] + [jax.ShapeDtypeStruct((n, TILE, width), jnp.float32) for n in sizes],
        in_specs=specs,
        out_specs=[rows_of(acc.shape)] + [pl.BlockSpec(memory_space=pl.ANY)] * len(sizes),
        scratch_shapes=scratch,
        compiler_params=pltpu.CompilerParams(vmem_limit_bytes=24 * MIB),
        cost_estimate=SMALL,
    )(*args)


def tie(values, *others):
    done = lax.optimization_barrier(tuple(values) + tuple(others))
    return list(done[: len(values)]), list(done[len(values) :])


def local(features, tile_rows, tile_cols, tile_vals, tile_count, near_send, far_send, skew_raw):
    width = features.shape[1]
    row_blocks = features.shape[0] // TILE
    peers, cap, hcap = near_send.shape[1], near_send.shape[2], far_send.shape[2]
    domains = lax.axis_size("dom")
    d = lax.axis_index("dev")
    me = d.astype(jnp.int32).reshape(1)

    late = list(range(peers // 4, peers // 2))[::-1]
    early = list(range(1, peers // 4))
    plan = tuple(
        [(("near", 2 * j), ("near", 2 * j + 1)) for j in late + early]
        + [(("far", 0),), (("far", 1),), (("near", 1),)]
    )
    route = (plan, me, near_send[0], far_send[0])

    first_k = [2 * j for j in early + late[:-1]] + [1] + [2 * j + 1 for j in early + late[:-1]]
    last_k = [2 * late[-1], 2 * late[-1] + 1]
    widths = (row_blocks, 2 * hcap + cap * len(first_k), cap * len(last_k))
    place_of = [0] * peers
    for at, k in enumerate(first_k + last_k):
        place_of[k] = row_blocks + 2 * hcap + at * cap
    slot = tile_cols
    near_at = slot - row_blocks
    source, item = near_at // cap, near_at % cap
    source_safe = jnp.clip(source, 0, peers - 1)
    near_place = jnp.take(jnp.array(place_of, jnp.int32), source_safe ^ d) + item
    self_place = jnp.take(near_send[0].reshape(-1), d * cap + item)
    near_place = jnp.where(source_safe == d, self_place, near_place)
    far_place = slot - row_blocks - peers * cap + row_blocks
    places = jnp.where(
        slot < row_blocks, slot, jnp.where(slot < row_blocks + peers * cap, near_place, far_place)
    ).astype(jnp.int32)

    own_a, first_a, last_a = dense_adjacency(tile_rows, places, tile_count, tile_vals, row_blocks, widths)

    def swap(x, k):
        return lax.ppermute(x, "dev", [(i, i ^ k) for i in range(peers)])

    up = [(i, (i + 1) % domains) for i in range(domains)]
    down = [(j, i) for i, j in up]

    def start(sends):
        chips = late + early
        near = [swap(s, 2 * j) for s, j in zip(sends, chips)]
        lower = lax.ppermute(sends[len(chips)], "dom", up)
        upper = lax.ppermute(sends[len(chips) + 1], "dom", down)
        return near[: len(late)], near[len(late) :], lower, upper, sends[-1]

    def arrive(flight, acc, square=()):
        long, short, lower, upper, to_core = flight
        *later, last = long
        (to_core, *near), (acc,) = tie([to_core] + short + later, acc)
        across = [swap(to_core, 1)] + [swap(r[cap:], 1) for r in near]
        arrived = [(lower, hcap), (upper, hcap)] + [(r, cap) for r in near + across]
        acc = apply_dense(first_a, arrived, acc, square)
        (last,), (acc,) = tie([last], acc)
        return acc, [(last, cap), (swap(last[cap:], 1), cap)]

    current = features.reshape(row_blocks, TILE, width)
    sends = pick(current, route)
    parts = weights(skew_raw)
    layers = skew_raw.shape[0]
    for layer in range(layers):
        flight = start(sends)
        skew, square = [(w, layer) for w in parts[:2]], [(w, layer) for w in parts[2:]]
        acc, arrived = arrive(flight, apply_dense(own_a, [(current, row_blocks)]))
        once, *sends = finish(last_a, arrived, acc, route)
        flight = start(sends)
        base = mix(current, once, apply_dense(own_a, [(once, row_blocks)]), skew, square)
        base, arrived = arrive(flight, base, square)
        current, *sends = finish(last_a, arrived, base, route, square, layer < layers - 1)
    return current.reshape(features.shape)


def solution(mesh):
    nodes = ("dom", "dev")
    in_specs = (
        P(nodes, None),
        P(nodes),
        P(nodes),
        P(nodes, None, None),
        P(nodes),
        P(nodes, None, None),
        P(nodes, None, None),
        P(),
    )
    return jax.shard_map(local, mesh=mesh, in_specs=in_specs, out_specs=P(nodes, None), check_vma=False)
```

```python
import functools

import jax
import jax.numpy as jnp
from jax import lax
from jax.experimental import pallas as pl
from jax.experimental.pallas import tpu as pltpu
from jax.sharding import PartitionSpec as P

TILE = 128
STEP = 4
MIB = 1024 * 1024
SMALL = pl.CostEstimate(flops=1, bytes_accessed=1, transcendentals=0)


def split(x):
    high = x.astype(jnp.bfloat16)
    return high, (x - high.astype(jnp.float32)).astype(jnp.bfloat16)


def dot3(a_high, a_low, b_high, b_low):
    dot = functools.partial(jnp.dot, preferred_element_type=jnp.float32)
    return dot(a_high, b_high) + (dot(a_high, b_low) + dot(a_low, b_high))


def smem():
    return pl.BlockSpec(memory_space=pltpu.SMEM)


def whole(shape):
    return pl.BlockSpec(shape, lambda i: (0,) * len(shape))


def of_layer(weight):
    array, layer = weight
    return pl.BlockSpec((None,) + array.shape[1:], lambda i: (layer, 0, 0))


def rows_of(shape):
    return pl.BlockSpec((STEP,) + shape[1:], lambda i: (i,) + (0,) * (len(shape) - 1))


def dense_kernel(rows_ref, cols_ref, count_ref, vals_ref, *refs):
    outs, total = refs[:-1], refs[-1]
    total[...] = jnp.zeros_like(total)

    def add(t, carry):
        total[rows_ref[t], cols_ref[t]] += vals_ref[t]
        return carry

    lax.fori_loop(0, count_ref[0], add, 0)

    def write(r, carry):
        first = 0
        for high_ref, low_ref in zip(outs[::2], outs[1::2]):
            for c in range(high_ref.shape[2] // TILE):
                high, low = split(total[r, first + c])
                high_ref[r, :, c * TILE : (c + 1) * TILE] = high
                low_ref[r, :, c * TILE : (c + 1) * TILE] = low
            first += high_ref.shape[2] // TILE
        return carry

    lax.fori_loop(0, total.shape[0], write, 0)


def dense_adjacency(tile_rows, places, tile_count, tile_vals, row_blocks, widths):
    vmem = pl.BlockSpec(memory_space=pltpu.VMEM)
    out_shape = []
    for w in widths:
        out_shape += [jax.ShapeDtypeStruct((row_blocks, TILE, w * TILE), jnp.bfloat16)] * 2
    need = 4 * TILE * TILE * (tile_vals.shape[0] + 2 * row_blocks * sum(widths))
    flat = pl.pallas_call(
        dense_kernel,
        out_shape=out_shape,
        in_specs=[smem(), smem(), smem(), vmem],
        out_specs=[vmem] * len(out_shape),
        scratch_shapes=[pltpu.VMEM((row_blocks, sum(widths), TILE, TILE), jnp.float32)],
        compiler_params=pltpu.CompilerParams(vmem_limit_bytes=need + 4 * MIB),
        cost_estimate=SMALL,
    )(tile_rows, places, tile_count, tile_vals)
    return [(flat[2 * g], flat[2 * g + 1]) for g in range(len(widths))]


def weights_kernel(raw_ref, *refs):
    raw = raw_ref[0]
    skew = 0.5 * (raw - raw.T)
    square = 0.5 * jnp.dot(
        skew, skew, precision=lax.Precision.HIGHEST, preferred_element_type=jnp.float32
    )
    for ref, part in zip(refs, split(skew) + split(square)):
        ref[0] = part


def weights(skew_raw):
    block = pl.BlockSpec((1,) + skew_raw.shape[1:], lambda i: (i, 0, 0))
    return pl.pallas_call(
        weights_kernel,
        grid=(skew_raw.shape[0],),
        out_shape=[jax.ShapeDtypeStruct(skew_raw.shape, jnp.bfloat16)] * 4,
        in_specs=[block],
        out_specs=[block] * 4,
        compiler_params=pltpu.CompilerParams(vmem_limit_bytes=24 * MIB),
        cost_estimate=SMALL,
    )(skew_raw)


def load_split(x_refs, high, low):
    at = 0
    for x_ref in x_refs:
        for b in range(x_ref.shape[0]):
            high[at : at + TILE, :], low[at : at + TILE, :] = split(x_ref[b])
            at += TILE


def flat_rows(ref):
    return ref[...].reshape(-1, ref.shape[-1])


def load_product(x_refs, square_refs, high, low):
    load_split(x_refs, high, low)
    if square_refs:
        product = dot3(high[...], low[...], square_refs[0][...], square_refs[1][...])
        high[...], low[...] = split(product)


def apply_kernel(n_x, has_acc, squared, ah_ref, al_ref, *refs):
    x_refs = refs[:n_x]
    acc_ref = refs[n_x] if has_acc else None
    square_refs = refs[-5:-3] if squared else ()
    o_ref, high, low = refs[-3:]

    @pl.when(pl.program_id(0) == 0)
    def _():
        load_product(x_refs, square_refs, high, low)

    out = dot3(flat_rows(ah_ref), flat_rows(al_ref), high[...], low[...])
    if has_acc:
        out = out + flat_rows(acc_ref)
    o_ref[...] = out.reshape(o_ref.shape)


def front(x, count):
    return whole((count,) + x.shape[1:])


def apply_dense(dense, xs, acc=None, square=()):
    ah, al = dense
    width = xs[0][0].shape[-1]
    out = jax.ShapeDtypeStruct((ah.shape[0], TILE, width), jnp.float32)
    depth = ah.shape[2]
    args = [ah, al] + [x for x, _ in xs]
    specs = [rows_of(ah.shape), rows_of(al.shape)] + [front(x, n) for x, n in xs]
    if acc is not None:
        args.append(acc)
        specs.append(rows_of(acc.shape))
    args += [q for q, _ in square]
    specs += [of_layer(q) for q in square]
    return pl.pallas_call(
        functools.partial(apply_kernel, len(xs), acc is not None, bool(square)),
        grid=(ah.shape[0] // STEP,),
        out_shape=out,
        in_specs=specs,
        out_specs=rows_of(out.shape),
        scratch_shapes=[pltpu.VMEM((depth, width), jnp.bfloat16)] * 2,
        compiler_params=pltpu.CompilerParams(vmem_limit_bytes=8 * MIB + 22 * depth * width),
        cost_estimate=SMALL,
    )(*args)


def mix_kernel(x_ref, once_ref, twice_ref, sh_ref, sl_ref, qh_ref, ql_ref, o_ref):
    out = flat_rows(x_ref) + dot3(*split(flat_rows(once_ref)), sh_ref[...], sl_ref[...])
    out = out + dot3(*split(flat_rows(twice_ref)), qh_ref[...], ql_ref[...])
    o_ref[...] = out.reshape(o_ref.shape)


def mix(x, once, twice, skew, square):
    block = rows_of(x.shape)
    factors = [*skew, *square]
    width = x.shape[-1]
    return pl.pallas_call(
        mix_kernel,
        grid=(x.shape[0] // STEP,),
        out_shape=jax.ShapeDtypeStruct(x.shape, jnp.float32),
        in_specs=[block] * 3 + [of_layer(w) for w in factors],
        out_specs=block,
        compiler_params=pltpu.CompilerParams(vmem_limit_bytes=24 * MIB),
        cost_estimate=SMALL,
    )(x, once, twice, *[w for w, _ in factors])


def picked(plan, me, near_ref, far_ref):
    for entries in plan:
        blocks = []
        for kind, index in entries:
            if kind == "near":
                peer = me ^ index
                blocks += [near_ref[peer, i] for i in range(near_ref.shape[1])]
            else:
                blocks += [far_ref[index, i] for i in range(far_ref.shape[1])]
        yield blocks


def copy_out(plan, me_ref, near_ref, far_ref, source, send_refs, sems):
    copies = []
    for ref, blocks in zip(send_refs, picked(plan, me_ref[0], near_ref, far_ref)):
        for i, block in enumerate(blocks):
            copies.append(pltpu.make_async_copy(source.at[block], ref.at[i], sems.at[len(copies)]))
            copies[-1].start()
    for copy in copies:
        copy.wait()


def plan_sizes(plan, near, far):
    return [sum(near.shape[1] if kind == "near" else far.shape[1] for kind, _ in e) for e in plan]


def pick_kernel(plan, me_ref, near_ref, far_ref, x_ref, *refs):
    copy_out(plan, me_ref, near_ref, far_ref, x_ref, refs[:-1], refs[-1])


def pick(x, route):
    plan, me, near, far = route
    sizes = plan_sizes(plan, near, far)
    hbm = pl.BlockSpec(memory_space=pl.ANY)
    return pl.pallas_call(
        functools.partial(pick_kernel, plan),
        out_shape=[jax.ShapeDtypeStruct((n,) + x.shape[1:], x.dtype) for n in sizes],
        in_specs=[smem()] * 3 + [pl.BlockSpec(memory_space=pltpu.VMEM)],
        out_specs=[hbm] * len(sizes),
        scratch_shapes=[pltpu.SemaphoreType.DMA((sum(sizes),))],
        compiler_params=pltpu.CompilerParams(vmem_limit_bytes=16 * MIB),
        cost_estimate=SMALL,
    )(me, near, far, x)


def finish_kernel(plan, n_x, squared, n_send, me_ref, near_ref, far_ref, ah_ref, al_ref, acc_ref, *refs):
    refs = list(refs)
    x_refs = [refs.pop(0) for _ in range(n_x)]
    square_refs = [refs.pop(0) for _ in range(2 * squared)]
    o_ref = refs.pop(0)
    send_refs = [refs.pop(0) for _ in range(n_send)]
    high, low = refs.pop(0), refs.pop(0)
    step = pl.program_id(0)

    @pl.when(step == 0)
    def _():
        load_product(x_refs, square_refs, high, low)

    out = dot3(flat_rows(ah_ref), flat_rows(al_ref), high[...], low[...]) + flat_rows(acc_ref)
    if squared:
        width = out.shape[1]
        even = lax.broadcasted_iota(jnp.int32, out.shape, 1) % 2 == 0
        after, before = pltpu.roll(out, width - 1, 1), pltpu.roll(out, 1, 1)
        out = jnp.where(even, jnp.minimum(out, after), jnp.maximum(out, before))
    out = out.reshape(o_ref.shape)
    o_ref[...] = out
    if n_send:
        kept, sems = refs
        kept[pl.ds(step * STEP, STEP)] = out

        @pl.when(step == pl.num_programs(0) - 1)
        def _():
            copy_out(plan, me_ref, near_ref, far_ref, kept, send_refs, sems)


def finish(dense, xs, acc, route, square=(), send=True):
    plan, me, near, far = route
    sizes = plan_sizes(plan, near, far) if send else []
    ah, al = dense
    depth, width = ah.shape[2], acc.shape[2]
    field = jax.ShapeDtypeStruct(acc.shape, jnp.float32)
    args = [me, near, far, ah, al, acc] + [x for x, _ in xs]
    specs = [smem()] * 3 + [rows_of(ah.shape), rows_of(al.shape), rows_of(acc.shape)]
    specs += [front(x, n) for x, n in xs]
    args += [q for q, _ in square]
    specs += [of_layer(q) for q in square]
    scratch = [pltpu.VMEM((depth, width), jnp.bfloat16)] * 2
    if send:
        scratch += [pltpu.VMEM(acc.shape, jnp.float32), pltpu.SemaphoreType.DMA((sum(sizes),))]
    return pl.pallas_call(
        functools.partial(finish_kernel, plan, len(xs), bool(square), len(sizes)),
        grid=(acc.shape[0] // STEP,),
        out_shape=[field] + [jax.ShapeDtypeStruct((n, TILE, width), jnp.float32) for n in sizes],
        in_specs=specs,
        out_specs=[rows_of(acc.shape)] + [pl.BlockSpec(memory_space=pl.ANY)] * len(sizes),
        scratch_shapes=scratch,
        compiler_params=pltpu.CompilerParams(vmem_limit_bytes=24 * MIB),
        cost_estimate=SMALL,
    )(*args)


def tie(values, *others):
    done = lax.optimization_barrier(tuple(values) + tuple(others))
    return list(done[: len(values)]), list(done[len(values) :])


def local(features, tile_rows, tile_cols, tile_vals, tile_count, near_send, far_send, skew_raw):
    width = features.shape[1]
    row_blocks = features.shape[0] // TILE
    peers, cap, hcap = near_send.shape[1], near_send.shape[2], far_send.shape[2]
    domains = lax.axis_size("dom")
    d = lax.axis_index("dev")
    me = d.astype(jnp.int32).reshape(1)

    late = list(range(peers // 4, peers // 2))[::-1]
    early = list(range(1, peers // 4))
    plan = tuple(
        [(("near", 2 * j), ("near", 2 * j + 1)) for j in late + early]
        + [(("far", 0),), (("far", 1),), (("near", 1),)]
    )
    route = (plan, me, near_send[0], far_send[0])

    first_k = [2 * j for j in late[:-1] + early] + [1] + [2 * j + 1 for j in late[:-1] + early]
    last_k = [2 * late[-1], 2 * late[-1] + 1]
    widths = (row_blocks, 2 * hcap + cap * len(first_k), cap * len(last_k))
    place_of = [0] * peers
    for at, k in enumerate(first_k + last_k):
        place_of[k] = row_blocks + 2 * hcap + at * cap
    slot = tile_cols
    near_at = slot - row_blocks
    source, item = near_at // cap, near_at % cap
    source_safe = jnp.clip(source, 0, peers - 1)
    near_place = jnp.take(jnp.array(place_of, jnp.int32), source_safe ^ d) + item
    self_place = jnp.take(near_send[0].reshape(-1), d * cap + item)
    near_place = jnp.where(source_safe == d, self_place, near_place)
    far_place = slot - row_blocks - peers * cap + row_blocks
    places = jnp.where(
        slot < row_blocks, slot, jnp.where(slot < row_blocks + peers * cap, near_place, far_place)
    ).astype(jnp.int32)

    own_a, first_a, last_a = dense_adjacency(tile_rows, places, tile_count, tile_vals, row_blocks, widths)

    def swap(x, k):
        return lax.ppermute(x, "dev", [(i, i ^ k) for i in range(peers)])

    up = [(i, (i + 1) % domains) for i in range(domains)]
    down = [(j, i) for i, j in up]

    def start(sends):
        chips = late + early
        near = [swap(s, 2 * j) for s, j in zip(sends, chips)]
        lower = lax.ppermute(sends[len(chips)], "dom", up)
        upper = lax.ppermute(sends[len(chips) + 1], "dom", down)
        return near[: len(late)], near[len(late) :], lower, upper, sends[-1]

    def arrive(flight, acc, square=()):
        long, short, lower, upper, to_core = flight
        *later, last = long
        (to_core, *near), (acc,) = tie([to_core] + later + short, acc)
        across = [swap(to_core, 1)] + [swap(r[cap:], 1) for r in near]
        arrived = [(lower, hcap), (upper, hcap)] + [(r, cap) for r in near + across]
        acc = apply_dense(first_a, arrived, acc, square)
        (last,), (acc,) = tie([last], acc)
        return acc, [(last, cap), (swap(last[cap:], 1), cap)]

    current = features.reshape(row_blocks, TILE, width)
    sends = pick(current, route)
    parts = weights(skew_raw)
    layers = skew_raw.shape[0]
    for layer in range(layers):
        flight = start(sends)
        skew, square = [(w, layer) for w in parts[:2]], [(w, layer) for w in parts[2:]]
        acc, arrived = arrive(flight, apply_dense(own_a, [(current, row_blocks)]))
        once, *sends = finish(last_a, arrived, acc, route)
        flight = start(sends)
        base = mix(current, once, apply_dense(own_a, [(once, row_blocks)]), skew, square)
        base, arrived = arrive(flight, base, square)
        current, *sends = finish(last_a, arrived, base, route, square, layer < layers - 1)
    return current.reshape(features.shape)


def solution(mesh):
    nodes = ("dom", "dev")
    in_specs = (
        P(nodes, None),
        P(nodes),
        P(nodes),
        P(nodes, None, None),
        P(nodes),
        P(nodes, None, None),
        P(nodes, None, None),
        P(),
    )
    return jax.shard_map(local, mesh=mesh, in_specs=in_specs, out_specs=P(nodes, None), check_vma=False)
```

```python
import functools

import jax
import jax.numpy as jnp
from jax import lax
from jax.experimental import pallas as pl
from jax.experimental.pallas import tpu as pltpu
from jax.sharding import PartitionSpec as P

TILE = 128
STEP = 4
MIB = 1024 * 1024
SMALL = pl.CostEstimate(flops=1, bytes_accessed=1, transcendentals=0)


def split(x):
    high = x.astype(jnp.bfloat16)
    return high, (x - high.astype(jnp.float32)).astype(jnp.bfloat16)


def dot3(a_high, a_low, b_high, b_low):
    dot = functools.partial(jnp.dot, preferred_element_type=jnp.float32)
    return dot(a_high, b_high) + (dot(a_high, b_low) + dot(a_low, b_high))


def smem():
    return pl.BlockSpec(memory_space=pltpu.SMEM)


def whole(shape):
    return pl.BlockSpec(shape, lambda i: (0,) * len(shape))


def of_layer(weight):
    array, layer = weight
    return pl.BlockSpec((None,) + array.shape[1:], lambda i: (layer, 0, 0))


def rows_of(shape, step=STEP):
    return pl.BlockSpec((step,) + shape[1:], lambda i: (i,) + (0,) * (len(shape) - 1))


def dense_kernel(rows_ref, cols_ref, count_ref, vals_ref, *refs):
    outs, total = refs[:-1], refs[-1]
    total[...] = jnp.zeros_like(total)

    def add(t, carry):
        total[rows_ref[t], cols_ref[t]] += vals_ref[t]
        return carry

    lax.fori_loop(0, count_ref[0], add, 0)

    def write(r, carry):
        first = 0
        for high_ref, low_ref in zip(outs[::2], outs[1::2]):
            for c in range(high_ref.shape[2] // TILE):
                high, low = split(total[r, first + c])
                high_ref[r, :, c * TILE : (c + 1) * TILE] = high
                low_ref[r, :, c * TILE : (c + 1) * TILE] = low
            first += high_ref.shape[2] // TILE
        return carry

    lax.fori_loop(0, total.shape[0], write, 0)


def dense_adjacency(tile_rows, places, tile_count, tile_vals, row_blocks, widths):
    vmem = pl.BlockSpec(memory_space=pltpu.VMEM)
    out_shape = []
    for w in widths:
        out_shape += [jax.ShapeDtypeStruct((row_blocks, TILE, w * TILE), jnp.bfloat16)] * 2
    need = 4 * TILE * TILE * (tile_vals.shape[0] + 2 * row_blocks * sum(widths))
    flat = pl.pallas_call(
        dense_kernel,
        out_shape=out_shape,
        in_specs=[smem(), smem(), smem(), vmem],
        out_specs=[vmem] * len(out_shape),
        scratch_shapes=[pltpu.VMEM((row_blocks, sum(widths), TILE, TILE), jnp.float32)],
        compiler_params=pltpu.CompilerParams(vmem_limit_bytes=need + 4 * MIB),
        cost_estimate=SMALL,
    )(tile_rows, places, tile_count, tile_vals)
    return [(flat[2 * g], flat[2 * g + 1]) for g in range(len(widths))]


def weights_kernel(raw_ref, *refs):
    raw = raw_ref[0]
    skew = 0.5 * (raw - raw.T)
    square = 0.5 * jnp.dot(
        skew, skew, precision=lax.Precision.HIGHEST, preferred_element_type=jnp.float32
    )
    for ref, part in zip(refs, split(skew) + split(square)):
        ref[0] = part


def weights(skew_raw):
    block = pl.BlockSpec((1,) + skew_raw.shape[1:], lambda i: (i, 0, 0))
    return pl.pallas_call(
        weights_kernel,
        grid=(skew_raw.shape[0],),
        out_shape=[jax.ShapeDtypeStruct(skew_raw.shape, jnp.bfloat16)] * 4,
        in_specs=[block],
        out_specs=[block] * 4,
        compiler_params=pltpu.CompilerParams(vmem_limit_bytes=24 * MIB),
        cost_estimate=SMALL,
    )(skew_raw)


def load_split(x_refs, high, low):
    at = 0
    for x_ref in x_refs:
        for b in range(x_ref.shape[0]):
            high[at : at + TILE, :], low[at : at + TILE, :] = split(x_ref[b])
            at += TILE


def flat_rows(ref):
    return ref[...].reshape(-1, ref.shape[-1])


def load_product(x_refs, square_refs, high, low):
    load_split(x_refs, high, low)
    if square_refs:
        product = dot3(high[...], low[...], square_refs[0][...], square_refs[1][...])
        high[...], low[...] = split(product)


def apply_kernel(n_x, has_acc, squared, ah_ref, al_ref, *refs):
    x_refs = refs[:n_x]
    acc_ref = refs[n_x] if has_acc else None
    square_refs = refs[-5:-3] if squared else ()
    o_ref, high, low = refs[-3:]

    @pl.when(pl.program_id(0) == 0)
    def _():
        load_product(x_refs, square_refs, high, low)

    out = dot3(flat_rows(ah_ref), flat_rows(al_ref), high[...], low[...])
    if has_acc:
        out = out + flat_rows(acc_ref)
    o_ref[...] = out.reshape(o_ref.shape)


def front(x, count):
    return whole((count,) + x.shape[1:])


def apply_dense(dense, xs, acc=None, square=()):
    ah, al = dense
    width = xs[0][0].shape[-1]
    out = jax.ShapeDtypeStruct((ah.shape[0], TILE, width), jnp.float32)
    depth = ah.shape[2]
    args = [ah, al] + [x for x, _ in xs]
    specs = [rows_of(ah.shape), rows_of(al.shape)] + [front(x, n) for x, n in xs]
    if acc is not None:
        args.append(acc)
        specs.append(rows_of(acc.shape))
    args += [q for q, _ in square]
    specs += [of_layer(q) for q in square]
    return pl.pallas_call(
        functools.partial(apply_kernel, len(xs), acc is not None, bool(square)),
        grid=(ah.shape[0] // STEP,),
        out_shape=out,
        in_specs=specs,
        out_specs=rows_of(out.shape),
        scratch_shapes=[pltpu.VMEM((depth, width), jnp.bfloat16)] * 2,
        compiler_params=pltpu.CompilerParams(vmem_limit_bytes=8 * MIB + 22 * depth * width),
        cost_estimate=SMALL,
    )(*args)


def mix_kernel(x_ref, once_ref, twice_ref, sh_ref, sl_ref, qh_ref, ql_ref, o_ref):
    out = flat_rows(x_ref) + dot3(*split(flat_rows(once_ref)), sh_ref[...], sl_ref[...])
    out = out + dot3(*split(flat_rows(twice_ref)), qh_ref[...], ql_ref[...])
    o_ref[...] = out.reshape(o_ref.shape)


def mix(x, once, twice, skew, square):
    block = rows_of(x.shape)
    factors = [*skew, *square]
    width = x.shape[-1]
    return pl.pallas_call(
        mix_kernel,
        grid=(x.shape[0] // STEP,),
        out_shape=jax.ShapeDtypeStruct(x.shape, jnp.float32),
        in_specs=[block] * 3 + [of_layer(w) for w in factors],
        out_specs=block,
        compiler_params=pltpu.CompilerParams(vmem_limit_bytes=24 * MIB),
        cost_estimate=SMALL,
    )(x, once, twice, *[w for w, _ in factors])


def picked(plan, me, near_ref, far_ref):
    for entries in plan:
        blocks = []
        for kind, index, count in entries:
            if kind == "near":
                peer = me ^ index
                blocks += [near_ref[peer * count + i] for i in range(count)]
            else:
                blocks += [far_ref[index, i] for i in range(count)]
        yield blocks


def copy_out(plan, me_ref, near_ref, far_ref, source, send_refs, sems):
    copies = []
    for ref, blocks in zip(send_refs, picked(plan, me_ref[0], near_ref, far_ref)):
        for i, block in enumerate(blocks):
            copies.append(pltpu.make_async_copy(source.at[block], ref.at[i], sems.at[len(copies)]))
            copies[-1].start()
    for copy in copies:
        copy.wait()


def plan_sizes(plan):
    return [sum(count for _, _, count in entries) for entries in plan]


def pick_kernel(plan, me_ref, near_ref, far_ref, x_ref, *refs):
    copy_out(plan, me_ref, near_ref, far_ref, x_ref, refs[:-1], refs[-1])


def pick(x, route):
    plan, me, near, far = route
    sizes = plan_sizes(plan)
    return pl.pallas_call(
        functools.partial(pick_kernel, plan),
        out_shape=[jax.ShapeDtypeStruct((n,) + x.shape[1:], x.dtype) for n in sizes],
        in_specs=[smem()] * 3 + [pl.BlockSpec(memory_space=pl.ANY)],
        out_specs=[pl.BlockSpec(memory_space=pltpu.VMEM)] * len(sizes),
        scratch_shapes=[pltpu.SemaphoreType.DMA((sum(sizes),))],
        compiler_params=pltpu.CompilerParams(vmem_limit_bytes=56 * MIB),
        cost_estimate=SMALL,
    )(me, near, far, x)


def finish_kernel(plan, n_x, squared, n_send, me_ref, near_ref, far_ref, ah_ref, al_ref, acc_ref, *refs):
    refs = list(refs)
    x_refs = [refs.pop(0) for _ in range(n_x)]
    square_refs = [refs.pop(0) for _ in range(2 * squared)]
    o_ref = refs.pop(0)
    send_refs = [refs.pop(0) for _ in range(n_send)]
    high, low = refs.pop(0), refs.pop(0)
    step = pl.program_id(0)

    @pl.when(step == 0)
    def _():
        load_product(x_refs, square_refs, high, low)

    out = dot3(flat_rows(ah_ref), flat_rows(al_ref), high[...], low[...]) + flat_rows(acc_ref)
    if squared:
        width = out.shape[1]
        even = lax.broadcasted_iota(jnp.int32, out.shape, 1) % 2 == 0
        after, before = pltpu.roll(out, width - 1, 1), pltpu.roll(out, 1, 1)
        out = jnp.where(even, jnp.minimum(out, after), jnp.maximum(out, before))
    out = out.reshape(o_ref.shape)
    o_ref[...] = out
    if n_send:
        kept, sems = refs
        kept[pl.ds(step * out.shape[0], out.shape[0])] = out

        @pl.when(step == pl.num_programs(0) - 1)
        def _():
            copy_out(plan, me_ref, near_ref, far_ref, kept, send_refs, sems)


def finish(dense, xs, acc, route, square=(), send=True):
    plan, me, near, far = route
    sizes = plan_sizes(plan) if send else []
    ah, al = dense
    step = acc.shape[0] if send else STEP
    depth, width = ah.shape[2], acc.shape[2]
    field = jax.ShapeDtypeStruct(acc.shape, jnp.float32)
    args = [me, near, far, ah, al, acc] + [x for x, _ in xs]
    specs = [smem()] * 3 + [rows_of(ah.shape, step), rows_of(al.shape, step), rows_of(acc.shape, step)]
    specs += [front(x, n) for x, n in xs]
    args += [q for q, _ in square]
    specs += [of_layer(q) for q in square]
    scratch = [pltpu.VMEM((depth, width), jnp.bfloat16)] * 2
    if send:
        scratch += [pltpu.VMEM(acc.shape, jnp.float32), pltpu.SemaphoreType.DMA((sum(sizes),))]
    return pl.pallas_call(
        functools.partial(finish_kernel, plan, len(xs), bool(square), len(sizes)),
        grid=(acc.shape[0] // step,),
        out_shape=[field] + [jax.ShapeDtypeStruct((n, TILE, width), jnp.float32) for n in sizes],
        in_specs=specs,
        out_specs=[rows_of(acc.shape, step)] + [pl.BlockSpec(memory_space=pl.ANY)] * len(sizes),
        scratch_shapes=scratch,
        compiler_params=pltpu.CompilerParams(vmem_limit_bytes=24 * MIB),
        cost_estimate=SMALL,
    )(*args)


def tie(values, *others):
    done = lax.optimization_barrier(tuple(values) + tuple(others))
    return list(done[: len(values)]), list(done[len(values) :])


def local(features, tile_rows, tile_cols, tile_vals, tile_count, near_send, far_send, skew_raw):
    width = features.shape[1]
    row_blocks = features.shape[0] // TILE
    peers, cap, hcap = near_send.shape[1], near_send.shape[2], far_send.shape[2]
    domains = lax.axis_size("dom")
    d = lax.axis_index("dev")
    me = d.astype(jnp.int32).reshape(1)

    late = list(range(peers // 4, peers // 2))[::-1]
    early = list(range(1, peers // 4))
    plan = tuple(
        [(("near", 2 * j, cap), ("near", 2 * j + 1, cap)) for j in late + early]
        + [(("far", 0, hcap),), (("far", 1, hcap),), (("near", 1, cap),)]
    )
    route = (plan, me, near_send.reshape(-1), far_send[0])

    first_k = [2 * j for j in late[:-1] + early] + [1] + [2 * j + 1 for j in late[:-1] + early]
    last_k = [2 * late[-1], 2 * late[-1] + 1]
    widths = (row_blocks, 2 * hcap + cap * len(first_k), cap * len(last_k))
    place_of = [0] * peers
    for at, k in enumerate(first_k + last_k):
        place_of[k] = row_blocks + 2 * hcap + at * cap
    slot = tile_cols
    near_at = slot - row_blocks
    source, item = near_at // cap, near_at % cap
    source_safe = jnp.clip(source, 0, peers - 1)
    near_place = jnp.take(jnp.array(place_of, jnp.int32), source_safe ^ d) + item
    self_place = jnp.take(near_send[0].reshape(-1), d * cap + item)
    near_place = jnp.where(source_safe == d, self_place, near_place)
    far_place = slot - row_blocks - peers * cap + row_blocks
    places = jnp.where(
        slot < row_blocks, slot, jnp.where(slot < row_blocks + peers * cap, near_place, far_place)
    ).astype(jnp.int32)

    own_a, first_a, last_a = dense_adjacency(tile_rows, places, tile_count, tile_vals, row_blocks, widths)

    def swap(x, k):
        return lax.ppermute(x, "dev", [(i, i ^ k) for i in range(peers)])

    up = [(i, (i + 1) % domains) for i in range(domains)]
    down = [(j, i) for i, j in up]

    def start(sends):
        chips = late + early
        near = [swap(s, 2 * j) for s, j in zip(sends, chips)]
        lower = lax.ppermute(sends[len(chips)], "dom", up)
        upper = lax.ppermute(sends[len(chips) + 1], "dom", down)
        return near[: len(late)], near[len(late) :], lower, upper, sends[-1]

    def arrive(flight, acc, square=()):
        long, short, lower, upper, to_core = flight
        *later, last = long
        (to_core, *near), (acc,) = tie([to_core] + later + short, acc)
        across = [swap(to_core, 1)] + [swap(r[cap:], 1) for r in near]
        arrived = [(lower, hcap), (upper, hcap)] + [(r, cap) for r in near + across]
        acc = apply_dense(first_a, arrived, acc, square)
        (last,), (acc,) = tie([last], acc)
        return acc, [(last, cap), (swap(last[cap:], 1), cap)]

    current = features.reshape(row_blocks, TILE, width)
    sends = pick(current, route)
    parts = weights(skew_raw)
    layers = skew_raw.shape[0]
    for layer in range(layers):
        flight = start(sends)
        skew, square = [(w, layer) for w in parts[:2]], [(w, layer) for w in parts[2:]]
        acc, arrived = arrive(flight, apply_dense(own_a, [(current, row_blocks)]))
        once, *sends = finish(last_a, arrived, acc, route)
        flight = start(sends)
        base = mix(current, once, apply_dense(own_a, [(once, row_blocks)]), skew, square)
        base, arrived = arrive(flight, base, square)
        current, *sends = finish(last_a, arrived, base, route, square, layer < layers - 1)
    return current.reshape(features.shape)


def solution(mesh):
    nodes = ("dom", "dev")
    in_specs = (
        P(nodes, None),
        P(nodes),
        P(nodes),
        P(nodes, None, None),
        P(nodes),
        P(nodes, None, None),
        P(nodes, None, None),
        P(),
    )
    return jax.shard_map(local, mesh=mesh, in_specs=in_specs, out_specs=P(nodes, None), check_vma=False)
```

```python
import functools

import jax
import jax.numpy as jnp
from jax import lax
from jax.experimental import pallas as pl
from jax.experimental.pallas import tpu as pltpu
from jax.sharding import PartitionSpec as P

TILE = 128
STEP = 4
MIB = 1024 * 1024
SMALL = pl.CostEstimate(flops=1, bytes_accessed=1, transcendentals=0)


def split(x):
    high = x.astype(jnp.bfloat16)
    return high, (x - high.astype(jnp.float32)).astype(jnp.bfloat16)


def dot3(a_high, a_low, b_high, b_low):
    dot = functools.partial(jnp.dot, preferred_element_type=jnp.float32)
    return dot(a_high, b_high) + (dot(a_high, b_low) + dot(a_low, b_high))


def smem():
    return pl.BlockSpec(memory_space=pltpu.SMEM)


def whole(shape):
    return pl.BlockSpec(shape, lambda i: (0,) * len(shape))


def of_layer(weight):
    array, layer = weight
    return pl.BlockSpec((None,) + array.shape[1:], lambda i: (layer, 0, 0))


def rows_of(shape, step=STEP):
    return pl.BlockSpec((step,) + shape[1:], lambda i: (i,) + (0,) * (len(shape) - 1))


def dense_kernel(rows_ref, cols_ref, count_ref, vals_ref, *refs):
    outs, total = refs[:-1], refs[-1]
    total[...] = jnp.zeros_like(total)

    def add(t, carry):
        total[rows_ref[t], cols_ref[t]] += vals_ref[t]
        return carry

    lax.fori_loop(0, count_ref[0], add, 0)

    def write(r, carry):
        first = 0
        for high_ref, low_ref in zip(outs[::2], outs[1::2]):
            for c in range(high_ref.shape[2] // TILE):
                high, low = split(total[r, first + c])
                high_ref[r, :, c * TILE : (c + 1) * TILE] = high
                low_ref[r, :, c * TILE : (c + 1) * TILE] = low
            first += high_ref.shape[2] // TILE
        return carry

    lax.fori_loop(0, total.shape[0], write, 0)


def dense_adjacency(tile_rows, places, tile_count, tile_vals, row_blocks, widths):
    vmem = pl.BlockSpec(memory_space=pltpu.VMEM)
    out_shape = []
    for w in widths:
        out_shape += [jax.ShapeDtypeStruct((row_blocks, TILE, w * TILE), jnp.bfloat16)] * 2
    need = 4 * TILE * TILE * (tile_vals.shape[0] + 2 * row_blocks * sum(widths))
    flat = pl.pallas_call(
        dense_kernel,
        out_shape=out_shape,
        in_specs=[smem(), smem(), smem(), vmem],
        out_specs=[vmem] * len(out_shape),
        scratch_shapes=[pltpu.VMEM((row_blocks, sum(widths), TILE, TILE), jnp.float32)],
        compiler_params=pltpu.CompilerParams(vmem_limit_bytes=need + 4 * MIB),
        cost_estimate=SMALL,
    )(tile_rows, places, tile_count, tile_vals)
    return [(flat[2 * g], flat[2 * g + 1]) for g in range(len(widths))]


def weights_kernel(raw_ref, *refs):
    raw = raw_ref[0]
    skew = 0.5 * (raw - raw.T)
    square = 0.5 * jnp.dot(
        skew, skew, precision=lax.Precision.HIGHEST, preferred_element_type=jnp.float32
    )
    for ref, part in zip(refs, split(skew) + split(square)):
        ref[0] = part


def weights(skew_raw):
    block = pl.BlockSpec((1,) + skew_raw.shape[1:], lambda i: (i, 0, 0))
    return pl.pallas_call(
        weights_kernel,
        grid=(skew_raw.shape[0],),
        out_shape=[jax.ShapeDtypeStruct(skew_raw.shape, jnp.bfloat16)] * 4,
        in_specs=[block],
        out_specs=[block] * 4,
        compiler_params=pltpu.CompilerParams(vmem_limit_bytes=24 * MIB),
        cost_estimate=SMALL,
    )(skew_raw)


def load_split(x_refs, high, low):
    at = 0
    for x_ref in x_refs:
        for b in range(x_ref.shape[0]):
            high[at : at + TILE, :], low[at : at + TILE, :] = split(x_ref[b])
            at += TILE


def flat_rows(ref):
    return ref[...].reshape(-1, ref.shape[-1])


def load_product(x_refs, square_refs, high, low):
    load_split(x_refs, high, low)
    if square_refs:
        product = dot3(high[...], low[...], square_refs[0][...], square_refs[1][...])
        high[...], low[...] = split(product)


def apply_kernel(n_x, has_acc, squared, ah_ref, al_ref, *refs):
    x_refs = refs[:n_x]
    acc_ref = refs[n_x] if has_acc else None
    square_refs = refs[-5:-3] if squared else ()
    o_ref, high, low = refs[-3:]

    @pl.when(pl.program_id(0) == 0)
    def _():
        load_product(x_refs, square_refs, high, low)

    out = dot3(flat_rows(ah_ref), flat_rows(al_ref), high[...], low[...])
    if has_acc:
        out = out + flat_rows(acc_ref)
    o_ref[...] = out.reshape(o_ref.shape)


def front(x, count):
    return whole((count,) + x.shape[1:])


def apply_dense(dense, xs, acc=None, square=()):
    ah, al = dense
    width = xs[0][0].shape[-1]
    out = jax.ShapeDtypeStruct((ah.shape[0], TILE, width), jnp.float32)
    depth = ah.shape[2]
    args = [ah, al] + [x for x, _ in xs]
    specs = [rows_of(ah.shape), rows_of(al.shape)] + [front(x, n) for x, n in xs]
    if acc is not None:
        args.append(acc)
        specs.append(rows_of(acc.shape))
    args += [q for q, _ in square]
    specs += [of_layer(q) for q in square]
    return pl.pallas_call(
        functools.partial(apply_kernel, len(xs), acc is not None, bool(square)),
        grid=(ah.shape[0] // STEP,),
        out_shape=out,
        in_specs=specs,
        out_specs=rows_of(out.shape),
        scratch_shapes=[pltpu.VMEM((depth, width), jnp.bfloat16)] * 2,
        compiler_params=pltpu.CompilerParams(vmem_limit_bytes=8 * MIB + 22 * depth * width),
        cost_estimate=SMALL,
    )(*args)


def mix_kernel(x_ref, once_ref, twice_ref, sh_ref, sl_ref, qh_ref, ql_ref, o_ref):
    out = flat_rows(x_ref) + dot3(*split(flat_rows(once_ref)), sh_ref[...], sl_ref[...])
    out = out + dot3(*split(flat_rows(twice_ref)), qh_ref[...], ql_ref[...])
    o_ref[...] = out.reshape(o_ref.shape)


def mix(x, once, twice, skew, square):
    block = rows_of(x.shape)
    factors = [*skew, *square]
    width = x.shape[-1]
    return pl.pallas_call(
        mix_kernel,
        grid=(x.shape[0] // STEP,),
        out_shape=jax.ShapeDtypeStruct(x.shape, jnp.float32),
        in_specs=[block] * 3 + [of_layer(w) for w in factors],
        out_specs=block,
        compiler_params=pltpu.CompilerParams(vmem_limit_bytes=24 * MIB),
        cost_estimate=SMALL,
    )(x, once, twice, *[w for w, _ in factors])


def picked(plan, me, near_ref, far_ref):
    for entries in plan:
        blocks = []
        for kind, index, count in entries:
            if kind == "near":
                peer = me ^ index
                blocks += [near_ref[peer * count + i] for i in range(count)]
            else:
                blocks += [far_ref[index, i] for i in range(count)]
        yield blocks


def copy_out(plan, me_ref, near_ref, far_ref, source, send_refs, sems):
    copies = []
    for ref, blocks in zip(send_refs, picked(plan, me_ref[0], near_ref, far_ref)):
        for i, block in enumerate(blocks):
            copies.append(pltpu.make_async_copy(source.at[block], ref.at[i], sems.at[len(copies)]))
            copies[-1].start()
    for copy in copies:
        copy.wait()


def plan_sizes(plan):
    return [sum(count for _, _, count in entries) for entries in plan]


def pick_kernel(plan, me_ref, near_ref, far_ref, x_ref, *refs):
    copy_out(plan, me_ref, near_ref, far_ref, x_ref, refs[:-1], refs[-1])


def pick(x, route):
    plan, me, near, far = route
    sizes = plan_sizes(plan)
    return pl.pallas_call(
        functools.partial(pick_kernel, plan),
        out_shape=[jax.ShapeDtypeStruct((n,) + x.shape[1:], x.dtype) for n in sizes],
        in_specs=[smem()] * 3 + [pl.BlockSpec(memory_space=pl.ANY)],
        out_specs=[pl.BlockSpec(memory_space=pltpu.VMEM)] * len(sizes),
        scratch_shapes=[pltpu.SemaphoreType.DMA((sum(sizes),))],
        compiler_params=pltpu.CompilerParams(vmem_limit_bytes=56 * MIB),
        cost_estimate=SMALL,
    )(me, near, far, x)


def finish_kernel(plan, n_x, squared, n_send, me_ref, near_ref, far_ref, ah_ref, al_ref, acc_ref, *refs):
    refs = list(refs)
    x_refs = [refs.pop(0) for _ in range(n_x)]
    square_refs = [refs.pop(0) for _ in range(2 * squared)]
    o_ref = refs.pop(0)
    send_refs = [refs.pop(0) for _ in range(n_send)]
    high, low = refs.pop(0), refs.pop(0)
    step = pl.program_id(0)

    @pl.when(step == 0)
    def _():
        load_product(x_refs, square_refs, high, low)

    out = dot3(flat_rows(ah_ref), flat_rows(al_ref), high[...], low[...]) + flat_rows(acc_ref)
    if squared:
        width = out.shape[1]
        even = lax.broadcasted_iota(jnp.int32, out.shape, 1) % 2 == 0
        after, before = pltpu.roll(out, width - 1, 1), pltpu.roll(out, 1, 1)
        out = jnp.where(even, jnp.minimum(out, after), jnp.maximum(out, before))
    out = out.reshape(o_ref.shape)
    o_ref[...] = out
    if n_send:
        kept, sems = refs
        kept[pl.ds(step * out.shape[0], out.shape[0])] = out

        @pl.when(step == pl.num_programs(0) - 1)
        def _():
            copy_out(plan, me_ref, near_ref, far_ref, kept, send_refs, sems)


def finish(dense, xs, acc, route, square=(), send=True):
    plan, me, near, far = route
    sizes = plan_sizes(plan) if send else []
    ah, al = dense
    step = acc.shape[0] if send else STEP
    depth, width = ah.shape[2], acc.shape[2]
    field = jax.ShapeDtypeStruct(acc.shape, jnp.float32)
    args = [me, near, far, ah, al, acc] + [x for x, _ in xs]
    specs = [smem()] * 3 + [rows_of(ah.shape, step), rows_of(al.shape, step), rows_of(acc.shape, step)]
    specs += [front(x, n) for x, n in xs]
    args += [q for q, _ in square]
    specs += [of_layer(q) for q in square]
    scratch = [pltpu.VMEM((depth, width), jnp.bfloat16)] * 2
    if send:
        scratch += [pltpu.VMEM(acc.shape, jnp.float32), pltpu.SemaphoreType.DMA((sum(sizes),))]
    return pl.pallas_call(
        functools.partial(finish_kernel, plan, len(xs), bool(square), len(sizes)),
        grid=(acc.shape[0] // step,),
        out_shape=[field] + [jax.ShapeDtypeStruct((n, TILE, width), jnp.float32) for n in sizes],
        in_specs=specs,
        out_specs=[rows_of(acc.shape, step)] + [pl.BlockSpec(memory_space=pl.ANY)] * len(sizes),
        scratch_shapes=scratch,
        compiler_params=pltpu.CompilerParams(vmem_limit_bytes=24 * MIB),
        cost_estimate=SMALL,
    )(*args)


def tie(values, *others):
    done = lax.optimization_barrier(tuple(values) + tuple(others))
    return list(done[: len(values)]), list(done[len(values) :])


def local(features, tile_rows, tile_cols, tile_vals, tile_count, near_send, far_send, skew_raw):
    width = features.shape[1]
    row_blocks = features.shape[0] // TILE
    peers, cap, hcap = near_send.shape[1], near_send.shape[2], far_send.shape[2]
    domains = lax.axis_size("dom")
    d = lax.axis_index("dev")
    me = d.astype(jnp.int32).reshape(1)

    late = list(range(peers // 4, peers // 2))[::-1]
    early = list(range(1, peers // 4))
    plan = tuple(
        [(("near", 2 * j, cap), ("near", 2 * j + 1, cap)) for j in late + early]
        + [(("far", 0, hcap),), (("far", 1, hcap),), (("near", 1, cap),)]
    )
    route = (plan, me, near_send.reshape(-1), far_send[0])

    first_k = [2 * j for j in late[:-1] + early] + [1] + [2 * j + 1 for j in late[:-1] + early]
    last_k = [2 * late[-1], 2 * late[-1] + 1]
    widths = (row_blocks, 2 * hcap + cap * len(first_k), cap * len(last_k))
    place_of = [0] * peers
    for at, k in enumerate(first_k + last_k):
        place_of[k] = row_blocks + 2 * hcap + at * cap
    slot = tile_cols
    near_at = slot - row_blocks
    source, item = near_at // cap, near_at % cap
    source_safe = jnp.clip(source, 0, peers - 1)
    near_place = jnp.take(jnp.array(place_of, jnp.int32), source_safe ^ d) + item
    self_place = jnp.take(near_send[0].reshape(-1), d * cap + item)
    near_place = jnp.where(source_safe == d, self_place, near_place)
    far_place = slot - row_blocks - peers * cap + row_blocks
    places = jnp.where(
        slot < row_blocks, slot, jnp.where(slot < row_blocks + peers * cap, near_place, far_place)
    ).astype(jnp.int32)

    own_a, first_a, last_a = dense_adjacency(tile_rows, places, tile_count, tile_vals, row_blocks, widths)

    def swap(x, k):
        return lax.ppermute(x, "dev", [(i, i ^ k) for i in range(peers)])

    up = [(i, (i + 1) % domains) for i in range(domains)]
    down = [(j, i) for i, j in up]

    def start(sends):
        chips = late + early
        near = [swap(s, 2 * j) for s, j in zip(sends, chips)]
        lower = lax.ppermute(sends[len(chips)], "dom", up)
        upper = lax.ppermute(sends[len(chips) + 1], "dom", down)
        return near[: len(late)], near[len(late) :], lower, upper, sends[-1]

    def arrive(flight, acc, square=()):
        long, short, lower, upper, to_core = flight
        *later, last = long
        (to_core, *near), (acc,) = tie([to_core] + later + short, acc)
        across = [swap(to_core, 1)] + [swap(r[cap:], 1) for r in near]
        arrived = [(lower, hcap), (upper, hcap)] + [(r, cap) for r in near + across]
        acc = apply_dense(first_a, arrived, acc, square)
        (last,), (acc,) = tie([last], acc)
        return acc, [(last, cap), (swap(last[cap:], 1), cap)]

    current = features.reshape(row_blocks, TILE, width)
    sends = pick(current, (plan[:1],) + route[1:]) + pick(current, (plan[1:],) + route[1:])
    parts = weights(skew_raw)
    layers = skew_raw.shape[0]
    for layer in range(layers):
        flight = start(sends)
        skew, square = [(w, layer) for w in parts[:2]], [(w, layer) for w in parts[2:]]
        acc, arrived = arrive(flight, apply_dense(own_a, [(current, row_blocks)]))
        once, *sends = finish(last_a, arrived, acc, route)
        flight = start(sends)
        base = mix(current, once, apply_dense(own_a, [(once, row_blocks)]), skew, square)
        base, arrived = arrive(flight, base, square)
        current, *sends = finish(last_a, arrived, base, route, square, layer < layers - 1)
    return current.reshape(features.shape)


def solution(mesh):
    nodes = ("dom", "dev")
    in_specs = (
        P(nodes, None),
        P(nodes),
        P(nodes),
        P(nodes, None, None),
        P(nodes),
        P(nodes, None, None),
        P(nodes, None, None),
        P(),
    )
    return jax.shard_map(local, mesh=mesh, in_specs=in_specs, out_specs=P(nodes, None), check_vma=False)
```

```python
import functools

import jax
import jax.numpy as jnp
from jax import lax
from jax.experimental import pallas as pl
from jax.experimental.pallas import tpu as pltpu
from jax.sharding import PartitionSpec as P

TILE = 128
STEP = 4
MIB = 1024 * 1024
SMALL = pl.CostEstimate(flops=1, bytes_accessed=1, transcendentals=0)


def split(x):
    high = x.astype(jnp.bfloat16)
    return high, (x - high.astype(jnp.float32)).astype(jnp.bfloat16)


def dot3(a_high, a_low, b_high, b_low):
    dot = functools.partial(jnp.dot, preferred_element_type=jnp.float32)
    return dot(a_high, b_high) + (dot(a_high, b_low) + dot(a_low, b_high))


def smem():
    return pl.BlockSpec(memory_space=pltpu.SMEM)


def whole(shape):
    return pl.BlockSpec(shape, lambda i: (0,) * len(shape))


def of_layer(weight):
    array, layer = weight
    return pl.BlockSpec((None,) + array.shape[1:], lambda i: (layer, 0, 0))


def rows_of(shape, step=STEP):
    return pl.BlockSpec((step,) + shape[1:], lambda i: (i,) + (0,) * (len(shape) - 1))


def dense_kernel(rows_ref, cols_ref, count_ref, vals_ref, *refs):
    outs, total = refs[:-1], refs[-1]
    total[...] = jnp.zeros_like(total)

    def add(t, carry):
        total[rows_ref[t], cols_ref[t]] += vals_ref[t]
        return carry

    lax.fori_loop(0, count_ref[0], add, 0)

    def write(r, carry):
        first = 0
        for high_ref, low_ref in zip(outs[::2], outs[1::2]):
            for c in range(high_ref.shape[2] // TILE):
                high, low = split(total[r, first + c])
                high_ref[r, :, c * TILE : (c + 1) * TILE] = high
                low_ref[r, :, c * TILE : (c + 1) * TILE] = low
            first += high_ref.shape[2] // TILE
        return carry

    lax.fori_loop(0, total.shape[0], write, 0)


def dense_adjacency(tile_rows, places, tile_count, tile_vals, row_blocks, widths):
    vmem = pl.BlockSpec(memory_space=pltpu.VMEM)
    out_shape = []
    for w in widths:
        out_shape += [jax.ShapeDtypeStruct((row_blocks, TILE, w * TILE), jnp.bfloat16)] * 2
    need = 4 * TILE * TILE * (tile_vals.shape[0] + 2 * row_blocks * sum(widths))
    flat = pl.pallas_call(
        dense_kernel,
        out_shape=out_shape,
        in_specs=[smem(), smem(), smem(), vmem],
        out_specs=[vmem] * len(out_shape),
        scratch_shapes=[pltpu.VMEM((row_blocks, sum(widths), TILE, TILE), jnp.float32)],
        compiler_params=pltpu.CompilerParams(vmem_limit_bytes=need + 4 * MIB),
        cost_estimate=SMALL,
    )(tile_rows, places, tile_count, tile_vals)
    return [(flat[2 * g], flat[2 * g + 1]) for g in range(len(widths))]


def weights_kernel(raw_ref, *refs):
    raw = raw_ref[0]
    skew = 0.5 * (raw - raw.T)
    square = 0.5 * jnp.dot(
        skew, skew, precision=lax.Precision.HIGHEST, preferred_element_type=jnp.float32
    )
    for ref, part in zip(refs, split(skew) + split(square)):
        ref[0] = part


def weights(skew_raw):
    block = pl.BlockSpec((1,) + skew_raw.shape[1:], lambda i: (i, 0, 0))
    return pl.pallas_call(
        weights_kernel,
        grid=(skew_raw.shape[0],),
        out_shape=[jax.ShapeDtypeStruct(skew_raw.shape, jnp.bfloat16)] * 4,
        in_specs=[block],
        out_specs=[block] * 4,
        compiler_params=pltpu.CompilerParams(vmem_limit_bytes=24 * MIB),
        cost_estimate=SMALL,
    )(skew_raw)


def load_split(x_refs, high, low):
    at = 0
    for x_ref in x_refs:
        for b in range(x_ref.shape[0]):
            high[at : at + TILE, :], low[at : at + TILE, :] = split(x_ref[b])
            at += TILE


def flat_rows(ref):
    return ref[...].reshape(-1, ref.shape[-1])


def load_product(x_refs, square_refs, high, low):
    load_split(x_refs, high, low)
    if square_refs:
        product = dot3(high[...], low[...], square_refs[0][...], square_refs[1][...])
        high[...], low[...] = split(product)


def apply_kernel(n_x, has_acc, squared, ah_ref, al_ref, *refs):
    x_refs = refs[:n_x]
    acc_ref = refs[n_x] if has_acc else None
    square_refs = refs[-5:-3] if squared else ()
    o_ref, high, low = refs[-3:]

    @pl.when(pl.program_id(0) == 0)
    def _():
        load_product(x_refs, square_refs, high, low)

    out = dot3(flat_rows(ah_ref), flat_rows(al_ref), high[...], low[...])
    if has_acc:
        out = out + flat_rows(acc_ref)
    o_ref[...] = out.reshape(o_ref.shape)


def front(x, count):
    return whole((count,) + x.shape[1:])


def apply_dense(dense, xs, acc=None, square=()):
    ah, al = dense
    width = xs[0][0].shape[-1]
    out = jax.ShapeDtypeStruct((ah.shape[0], TILE, width), jnp.float32)
    depth = ah.shape[2]
    args = [ah, al] + [x for x, _ in xs]
    specs = [rows_of(ah.shape), rows_of(al.shape)] + [front(x, n) for x, n in xs]
    if acc is not None:
        args.append(acc)
        specs.append(rows_of(acc.shape))
    args += [q for q, _ in square]
    specs += [of_layer(q) for q in square]
    return pl.pallas_call(
        functools.partial(apply_kernel, len(xs), acc is not None, bool(square)),
        grid=(ah.shape[0] // STEP,),
        out_shape=out,
        in_specs=specs,
        out_specs=rows_of(out.shape),
        scratch_shapes=[pltpu.VMEM((depth, width), jnp.bfloat16)] * 2,
        compiler_params=pltpu.CompilerParams(vmem_limit_bytes=8 * MIB + 22 * depth * width),
        cost_estimate=SMALL,
    )(*args)


def mix_kernel(x_ref, once_ref, twice_ref, sh_ref, sl_ref, qh_ref, ql_ref, o_ref):
    out = flat_rows(x_ref) + dot3(*split(flat_rows(once_ref)), sh_ref[...], sl_ref[...])
    out = out + dot3(*split(flat_rows(twice_ref)), qh_ref[...], ql_ref[...])
    o_ref[...] = out.reshape(o_ref.shape)


def mix(x, once, twice, skew, square):
    block = rows_of(x.shape)
    factors = [*skew, *square]
    width = x.shape[-1]
    return pl.pallas_call(
        mix_kernel,
        grid=(x.shape[0] // STEP,),
        out_shape=jax.ShapeDtypeStruct(x.shape, jnp.float32),
        in_specs=[block] * 3 + [of_layer(w) for w in factors],
        out_specs=block,
        compiler_params=pltpu.CompilerParams(vmem_limit_bytes=24 * MIB),
        cost_estimate=SMALL,
    )(x, once, twice, *[w for w, _ in factors])


def picked(plan, me, near_ref, far_ref):
    for entries in plan:
        blocks = []
        for kind, index, count in entries:
            if kind == "near":
                peer = me ^ index
                blocks += [near_ref[peer * count + i] for i in range(count)]
            else:
                blocks += [far_ref[index, i] for i in range(count)]
        yield blocks


def copy_out(plan, me_ref, near_ref, far_ref, source, send_refs, sems):
    copies = []
    for ref, blocks in zip(send_refs, picked(plan, me_ref[0], near_ref, far_ref)):
        for i, block in enumerate(blocks):
            copies.append(pltpu.make_async_copy(source.at[block], ref.at[i], sems.at[len(copies)]))
            copies[-1].start()
    for copy in copies:
        copy.wait()


def plan_sizes(plan):
    return [sum(count for _, _, count in entries) for entries in plan]


def pick_kernel(plan, me_ref, near_ref, far_ref, x_ref, *refs):
    copy_out(plan, me_ref, near_ref, far_ref, x_ref, refs[:-1], refs[-1])


def pick(x, route, space, limit):
    plan, me, near, far = route
    sizes = plan_sizes(plan)
    return pl.pallas_call(
        functools.partial(pick_kernel, plan),
        out_shape=[jax.ShapeDtypeStruct((n,) + x.shape[1:], x.dtype) for n in sizes],
        in_specs=[smem()] * 3 + [pl.BlockSpec(memory_space=space)],
        out_specs=[pl.BlockSpec(memory_space=pltpu.VMEM if space == pl.ANY else pl.ANY)] * len(sizes),
        scratch_shapes=[pltpu.SemaphoreType.DMA((sum(sizes),))],
        compiler_params=pltpu.CompilerParams(vmem_limit_bytes=limit * MIB),
        cost_estimate=SMALL,
    )(me, near, far, x)


def finish_kernel(plan, n_x, squared, n_send, me_ref, near_ref, far_ref, ah_ref, al_ref, acc_ref, *refs):
    refs = list(refs)
    x_refs = [refs.pop(0) for _ in range(n_x)]
    square_refs = [refs.pop(0) for _ in range(2 * squared)]
    o_ref = refs.pop(0)
    send_refs = [refs.pop(0) for _ in range(n_send)]
    high, low = refs.pop(0), refs.pop(0)
    step = pl.program_id(0)

    @pl.when(step == 0)
    def _():
        load_product(x_refs, square_refs, high, low)

    out = dot3(flat_rows(ah_ref), flat_rows(al_ref), high[...], low[...]) + flat_rows(acc_ref)
    if squared:
        width = out.shape[1]
        even = lax.broadcasted_iota(jnp.int32, out.shape, 1) % 2 == 0
        after, before = pltpu.roll(out, width - 1, 1), pltpu.roll(out, 1, 1)
        out = jnp.where(even, jnp.minimum(out, after), jnp.maximum(out, before))
    out = out.reshape(o_ref.shape)
    o_ref[...] = out
    if n_send:
        kept, sems = refs
        kept[pl.ds(step * out.shape[0], out.shape[0])] = out

        @pl.when(step == pl.num_programs(0) - 1)
        def _():
            copy_out(plan, me_ref, near_ref, far_ref, kept, send_refs, sems)


def finish(dense, xs, acc, route, square=(), send=True):
    plan, me, near, far = route
    sizes = plan_sizes(plan) if send else []
    ah, al = dense
    step = acc.shape[0] if send else STEP
    depth, width = ah.shape[2], acc.shape[2]
    field = jax.ShapeDtypeStruct(acc.shape, jnp.float32)
    args = [me, near, far, ah, al, acc] + [x for x, _ in xs]
    specs = [smem()] * 3 + [rows_of(ah.shape, step), rows_of(al.shape, step), rows_of(acc.shape, step)]
    specs += [front(x, n) for x, n in xs]
    args += [q for q, _ in square]
    specs += [of_layer(q) for q in square]
    scratch = [pltpu.VMEM((depth, width), jnp.bfloat16)] * 2
    if send:
        scratch += [pltpu.VMEM(acc.shape, jnp.float32), pltpu.SemaphoreType.DMA((sum(sizes),))]
    return pl.pallas_call(
        functools.partial(finish_kernel, plan, len(xs), bool(square), len(sizes)),
        grid=(acc.shape[0] // step,),
        out_shape=[field] + [jax.ShapeDtypeStruct((n, TILE, width), jnp.float32) for n in sizes],
        in_specs=specs,
        out_specs=[rows_of(acc.shape, step)] + [pl.BlockSpec(memory_space=pl.ANY)] * len(sizes),
        scratch_shapes=scratch,
        compiler_params=pltpu.CompilerParams(vmem_limit_bytes=24 * MIB),
        cost_estimate=SMALL,
    )(*args)


def tie(values, *others):
    done = lax.optimization_barrier(tuple(values) + tuple(others))
    return list(done[: len(values)]), list(done[len(values) :])


def local(features, tile_rows, tile_cols, tile_vals, tile_count, near_send, far_send, skew_raw):
    width = features.shape[1]
    row_blocks = features.shape[0] // TILE
    peers, cap, hcap = near_send.shape[1], near_send.shape[2], far_send.shape[2]
    domains = lax.axis_size("dom")
    d = lax.axis_index("dev")
    me = d.astype(jnp.int32).reshape(1)

    late = list(range(peers // 4, peers // 2))[::-1]
    early = list(range(1, peers // 4))
    plan = tuple(
        [(("near", 2 * j, cap), ("near", 2 * j + 1, cap)) for j in late + early]
        + [(("far", 0, hcap),), (("far", 1, hcap),), (("near", 1, cap),)]
    )
    route = (plan, me, near_send.reshape(-1), far_send[0])

    first_k = [2 * j for j in late[:-1] + early] + [1] + [2 * j + 1 for j in late[:-1] + early]
    last_k = [2 * late[-1], 2 * late[-1] + 1]
    widths = (row_blocks, 2 * hcap + cap * len(first_k), cap * len(last_k))
    place_of = [0] * peers
    for at, k in enumerate(first_k + last_k):
        place_of[k] = row_blocks + 2 * hcap + at * cap
    slot = tile_cols
    near_at = slot - row_blocks
    source, item = near_at // cap, near_at % cap
    source_safe = jnp.clip(source, 0, peers - 1)
    near_place = jnp.take(jnp.array(place_of, jnp.int32), source_safe ^ d) + item
    self_place = jnp.take(near_send[0].reshape(-1), d * cap + item)
    near_place = jnp.where(source_safe == d, self_place, near_place)
    far_place = slot - row_blocks - peers * cap + row_blocks
    places = jnp.where(
        slot < row_blocks, slot, jnp.where(slot < row_blocks + peers * cap, near_place, far_place)
    ).astype(jnp.int32)

    own_a, first_a, last_a = dense_adjacency(tile_rows, places, tile_count, tile_vals, row_blocks, widths)

    def swap(x, k):
        return lax.ppermute(x, "dev", [(i, i ^ k) for i in range(peers)])

    up = [(i, (i + 1) % domains) for i in range(domains)]
    down = [(j, i) for i, j in up]

    def start(sends):
        chips = late + early
        near = [swap(s, 2 * j) for s, j in zip(sends, chips)]
        lower = lax.ppermute(sends[len(chips)], "dom", up)
        upper = lax.ppermute(sends[len(chips) + 1], "dom", down)
        return near[: len(late)], near[len(late) :], lower, upper, sends[-1]

    def arrive(flight, acc, square=()):
        long, short, lower, upper, to_core = flight
        *later, last = long
        (to_core, *near), (acc,) = tie([to_core] + later + short, acc)
        across = [swap(to_core, 1)] + [swap(r[cap:], 1) for r in near]
        arrived = [(lower, hcap), (upper, hcap)] + [(r, cap) for r in near + across]
        acc = apply_dense(first_a, arrived, acc, square)
        (last,), (acc,) = tie([last], acc)
        return acc, [(last, cap), (swap(last[cap:], 1), cap)]

    current = features.reshape(row_blocks, TILE, width)
    sends = pick(current, (plan[:1],) + route[1:], pl.ANY, 56)
    sends += pick(current, (plan[1:],) + route[1:], pltpu.VMEM, 16)
    parts = weights(skew_raw)
    layers = skew_raw.shape[0]
    for layer in range(layers):
        flight = start(sends)
        skew, square = [(w, layer) for w in parts[:2]], [(w, layer) for w in parts[2:]]
        acc, arrived = arrive(flight, apply_dense(own_a, [(current, row_blocks)]))
        once, *sends = finish(last_a, arrived, acc, route)
        flight = start(sends)
        base = mix(current, once, apply_dense(own_a, [(once, row_blocks)]), skew, square)
        base, arrived = arrive(flight, base, square)
        current, *sends = finish(last_a, arrived, base, route, square, layer < layers - 1)
    return current.reshape(features.shape)


def solution(mesh):
    nodes = ("dom", "dev")
    in_specs = (
        P(nodes, None),
        P(nodes),
        P(nodes),
        P(nodes, None, None),
        P(nodes),
        P(nodes, None, None),
        P(nodes, None, None),
        P(),
    )
    return jax.shard_map(local, mesh=mesh, in_specs=in_specs, out_specs=P(nodes, None), check_vma=False)
```
